32 devices in a mesh: groups: 2 (over y), brick: 4 (over z), segment: 2 (over x), chan: 2 (over core).
Axes of the slice: x: 2, y: 2, z: 4, core: 2. Of those that a mesh axis runs over, the one named last changes fastest.
Arguments:
- saved_inputs: bfloat16 [2, 1, 96, 1024], P('segment', None, 'chan', ('groups', 'brick')), parts along dimension 3, may hold values from -6 to 6
- cotangent: bfloat16 [1, 96, 1024], P(None, 'chan', ('groups', 'brick')), parts along dimension 2, may hold values from -6 to 6
- weights: bfloat16 [2, 27, 9216], P('segment', None, 'chan'), may hold values from -0.0625 to 0.0625
- neighbors: int32 [1, 27, 1024], P(None, None, ('groups', 'brick')), parts along dimension 2, may hold values from 0 to 160, as said below
- send_lists: int32 [1, 8, 4, 8], P(None, ('groups', 'brick')), parts along dimension 1, may hold values from 0 to 127
Outputs:
- input_grads: bfloat16 [2, 1, 96, 1024], P('segment', None, 'chan', ('groups', 'brick')), parts along dimension 3
- weight_grads: float32 [4, 27, 9216], P(('groups', 'segment'), None, 'chan'), parts along dimension 0
The draws below stay inside these ranges and needn't reach their ends.
There are 2 independent parts, one for each index of `groups`. The reference program is written for one: setup_inputs(seed, part) draws one part's arguments, and reference() takes and returns one part's arrays. A program takes and returns all parts, laid end to end along the dimension named above; an argument that names none is the same for every part. Nothing has to cross between parts.
Inputs may be any that keep to these rules, and one draw needn't show every extreme that they name: `neighbors`: the code at offset 27 // 2 is the voxel's own local row. Codes reach the no-neighbour value in every draw.
All inputs are finite; a program needn't handle non-finite values.
Results may differ from the reference program's by a relative error of at most 0.0095.
Values may be sent and summed in bfloat16 or wider, within the bound.
A program may use at most 64 MiB of HBM per device.

```python
import jax
import jax.numpy as jnp
from jax import lax

CHANNELS = 96
TAPS = 27
ROWS_DEV = 128
HS = 8
MICRO = 1
LAYERS = 2
OWNERS = 4
TOTAL = 512


def draw_neighbors(key, part):
    shape = (MICRO, TAPS, TOTAL)
    choose = jax.random.randint(jax.random.fold_in(key, 11), shape, 0, 100)
    local_row = jax.random.randint(jax.random.fold_in(key, 12), shape, 0, ROWS_DEV)
    slot_pick = jax.random.randint(jax.random.fold_in(key, 13), shape, 0, OWNERS * HS)
    device_of = (jnp.arange(TOTAL, dtype=jnp.int32) // ROWS_DEV)[None, None, :]
    local_cut = 40 + device_of * 30 // max(OWNERS - 1, 1)
    halo_cut = local_cut + 25
    sentinel = ROWS_DEV + OWNERS * HS
    value = jnp.where(choose < local_cut, local_row, jnp.where(choose < halo_cut, ROWS_DEV + slot_pick, sentinel))
    own_row = (jnp.arange(TOTAL, dtype=jnp.int32) % ROWS_DEV)[None, None, :]
    tap_ids = jnp.arange(TAPS, dtype=jnp.int32)[None, :, None]
    return jnp.where(tap_ids == TAPS // 2, own_row, value).astype(jnp.int32)


def with_ends(drawn, own_key, low, largest):
    longest = drawn.shape.index(max(drawn.shape))
    spots = []
    for shift in (0, 1):
        where = [jax.random.randint(jax.random.fold_in(own_key, axis), (), 0, length) for axis, length in enumerate(drawn.shape)]
        where[longest] = (where[longest] + shift) % drawn.shape[longest]
        spots.append(tuple(where))
    return drawn.at[spots[0]].set(low).at[spots[1]].set(largest)


def levels(stream_key, extent, shards, smallest, top_value):
    level, own = 1.0, jax.random.fold_in(stream_key, 6)
    for position, shards_of in shards:
        heights = jnp.exp(jax.random.uniform(jax.random.fold_in(own, position), (shards_of,), jnp.float32, smallest / len(shards), top_value / len(shards)))
        level = level * jnp.repeat(heights, extent[position] // shards_of).reshape([-1 if axis == position else 1 for axis in range(len(extent))])
    return level


def bell_draw(own_key, dims, width, bound, split=(), kind=jnp.bfloat16):
    level = levels(own_key, dims, split, -0.22, 0.18) if split else 1.0
    entries = jax.random.normal(own_key, dims, jnp.float32) * width * level
    return jnp.minimum(jnp.maximum(entries, -bound), bound).astype(kind)


def setup_inputs(seed: int = 0, part: int = 0) -> dict:
    streams_of = jax.random.split(jax.random.key(seed), 6)
    part_keys = jax.random.split(jax.random.fold_in(streams_of[5], part), 6)
    saved_inputs = bell_draw(part_keys[0], (LAYERS, MICRO, CHANNELS, TOTAL), 1.0, 6.0, ((0, 2), (2, 2), (3, 4)))
    cotangent = bell_draw(part_keys[1], (MICRO, CHANNELS, TOTAL), 1.0, 6.0, ((1, 2), (2, 4)))
    weights = bell_draw(streams_of[2], (LAYERS, TAPS, CHANNELS * CHANNELS), (4 * TAPS * CHANNELS) ** -0.5, 0.0625, ((0, 2), (2, 2)))
    neighbors = draw_neighbors(jax.random.fold_in(jax.random.fold_in(streams_of[5], part), 71), part)
    send_lists = with_ends(jax.random.randint(part_keys[4], (MICRO, OWNERS, OWNERS, HS), 0, ROWS_DEV), jax.random.fold_in(part_keys[4], 1), 0, ROWS_DEV - 1).astype(jnp.int32)
    return {"saved_inputs": saved_inputs, "cotangent": cotangent, "weights": weights, "neighbors": neighbors, "send_lists": send_lists}


def global_codes(neighbors, send_lists):
    device_of = (jnp.arange(TOTAL, dtype=jnp.int32) // ROWS_DEV)[None, :]
    device_of = jnp.broadcast_to(device_of, (TAPS, TOTAL))
    limit = OWNERS * HS
    result = []
    for micro_id in range(MICRO):
        codes = neighbors[micro_id]
        is_local = codes < ROWS_DEV
        is_halo = jnp.logical_and(codes >= ROWS_DEV, codes < ROWS_DEV + limit)
        slot_code = jnp.clip(codes - ROWS_DEV, 0, limit - 1)
        source = slot_code // HS
        slot_id = slot_code % HS
        remote = send_lists[micro_id][source, device_of, slot_id]
        local_id = device_of * ROWS_DEV + jnp.clip(codes, 0, ROWS_DEV - 1)
        glob = jnp.where(is_local, local_id, jnp.where(is_halo, source * ROWS_DEV + remote, TOTAL))
        result.append(glob.astype(jnp.int32))
    return result


def reference(saved_inputs, cotangent, weights, neighbors, send_lists):
    codes = global_codes(neighbors, send_lists)
    high = lax.Precision.HIGHEST
    grads = [cotangent[micro_id] for micro_id in range(MICRO)]
    layer_outs = [None] * LAYERS
    weight_outs = [None] * LAYERS
    for layer in reversed(range(LAYERS)):
        kernel = jnp.transpose(weights[layer].astype(jnp.float32).reshape(TAPS, CHANNELS, CHANNELS), (0, 2, 1))
        grad_kernel = jnp.zeros((TAPS, CHANNELS, CHANNELS), jnp.float32)
        new_grads = []
        for micro_id in range(MICRO):
            padded = jnp.concatenate([saved_inputs[layer, micro_id], jnp.zeros((CHANNELS, 1), jnp.bfloat16)], axis=1)
            tap_rows = padded[:, codes[micro_id]].astype(jnp.float32)
            pre_act = jnp.einsum("ikt,kio->ot", tap_rows, kernel, precision=high)
            sigmoid_val = jax.nn.sigmoid(pre_act)
            upstream = grads[micro_id].astype(jnp.float32)
            grad_pre = (upstream * sigmoid_val * (1.0 + pre_act * (1.0 - sigmoid_val))).astype(jnp.bfloat16)
            grad_wide = grad_pre.astype(jnp.float32)
            grad_kernel = grad_kernel + jnp.einsum("ikt,ot->koi", tap_rows, grad_wide, precision=high)
            contrib = jnp.einsum("kio,ot->ikt", kernel, grad_wide, precision=high)
            conv_grad = jnp.zeros((CHANNELS, TOTAL + 1), jnp.float32).at[:, codes[micro_id]].add(contrib)[:, :TOTAL]
            new_grads.append((upstream + conv_grad).astype(jnp.bfloat16))
        grads = new_grads
        layer_outs[layer] = jnp.stack(new_grads, axis=0)
        weight_outs[layer] = grad_kernel.reshape(TAPS, CHANNELS * CHANNELS)
    return jnp.stack(layer_outs, axis=0), jnp.stack(weight_outs, axis=0)
```

```python
import functools
import math

import jax
import jax.numpy as jnp
from jax import lax
from jax.experimental import pallas as pl
from jax.experimental.pallas import tpu as pltpu
from jax.sharding import PartitionSpec as P

MESH = pl.DeviceIdType.MESH
F32 = jnp.float32
BF16 = jnp.bfloat16


def round_up(value, unit):
    return -(-value // unit) * unit


def dot(a, b, dims=((1,), (0,))):
    return lax.dot_general(a, b, (dims, ((), ())), preferred_element_type=F32)


def body(
    sizes,
    x_ref, cot_ref, w_ref, code_ref, list_ref,
    out_ref, dw_ref,
    xs, meta, w_rows, w_flat, w_turn, hot, taps, factor, up_buf, g_in, g_out, gp, gs,
    halo_out, halo_in, part_out, part_in, half_own,
    x_send, x_recv, m_send, m_recv, p_send, p_recv, h_send, h_recv,
    l_send, l_recv, s_send, s_recv,
):
    owners, chans, segments, half, full, rows, slots, tap_count = sizes
    peers = owners * chans
    ext = rows + owners * slots
    code_rows = round_up(tap_count, 8)
    stride = round_up(tap_count, 8)
    me = lax.axis_index("brick")
    ch = lax.axis_index("chan")
    seg = lax.axis_index("segment")
    top = seg == segments - 1
    mine = me * chans + ch

    def peer(step):
        other = lax.rem(mine + step, peers)
        return other, other // chans, lax.rem(other, chans)

    def brick(step):
        return lax.rem(me + step, owners)

    barrier = pltpu.get_barrier_semaphore()
    for step in range(1, peers):
        _, b, c = peer(step)
        pl.semaphore_signal(barrier, 1, device_id={"brick": b, "chan": c}, device_id_type=MESH)

    @pl.when(seg > 0)
    def _():
        pl.semaphore_signal(barrier, 1, device_id={"segment": seg - 1}, device_id_type=MESH)

    @pl.when(seg < segments - 1)
    def _():
        pl.semaphore_signal(barrier, 1, device_id={"segment": seg + 1}, device_id_type=MESH)

    lanes = lax.broadcasted_iota(jnp.int32, (owners, 128), 1)
    listed = jnp.concatenate([list_ref[0, 0]] * (128 // slots), axis=1)
    is_mine = lanes // slots == me
    meta[me, 0:tap_count, :] = code_ref[0]
    meta[me, code_rows : code_rows + owners, :] = jnp.where(is_mine, listed + me * rows, 0)
    own_list = jnp.where(is_mine, listed, -1)

    neighbours = (
        peers - 1 + jnp.where(seg > 0, 1, 0) + jnp.where(seg < segments - 1, 1, 0)
    )
    pl.semaphore_wait(barrier, neighbours)

    copies = []
    for step in range(1, peers):
        _, b, c = peer(step)
        copies.append(pltpu.make_async_remote_copy(
            src_ref=x_ref.at[0, 0], dst_ref=xs.at[mine],
            send_sem=x_send.at[step], recv_sem=x_recv.at[mine],
            device_id={"brick": b, "chan": c}, device_id_type=MESH))
        copies[-1].start()
    for step in range(1, owners):
        copies.append(pltpu.make_async_remote_copy(
            src_ref=meta.at[me], dst_ref=meta.at[me],
            send_sem=m_send.at[step], recv_sem=m_recv.at[me],
            device_id={"brick": brick(step)}, device_id_type=MESH))
        copies[-1].start()
    xs[mine] = x_ref[0, 0]

    group = math.lcm(full, 128) // full
    for first in range(0, half, group):
        count = min(group, half - first)
        block = w_ref[0, :, first * full : (first + count) * full].astype(F32)
        for j in range(count):
            at = (first + j) * stride
            w_rows[at : at + tap_count, 0:full] = block[:, j * full : (j + 1) * full]
    for k in range(tap_count):
        w_flat[k * half : (k + 1) * half, :] = (
            w_rows[pl.ds(k, half, stride=stride), :].astype(BF16)
        )
    w_turn[...] = jnp.transpose(w_flat[:, 0:full].astype(F32)).astype(BF16)

    ext_iota = lax.broadcasted_iota(jnp.int32, (ext, rows), 0)

    def one_hot(codes_of, k):
        return jnp.where(codes_of[k : k + 1, :] == ext_iota, 1.0, 0.0).astype(BF16)

    codes = code_ref[0]
    for k in range(tap_count):
        hot[:, k * rows : (k + 1) * rows] = one_hot(codes, k)

    def wait_slot(dst, sem):
        pltpu.make_async_copy(dst, dst, sem).wait()

    for step in range(1, peers):
        other, _, _ = peer(step)
        wait_slot(xs.at[other], x_recv.at[other])
    for step in range(1, owners):
        other = brick(step)
        wait_slot(meta.at[other], m_recv.at[other])

    def features(q):
        return jnp.concatenate([xs[q * chans + c] for c in range(chans)], axis=0)

    def extended(q):
        every = jnp.concatenate([features(o) for o in range(owners)], axis=1)
        row = meta[0, pl.ds(code_rows + q, 1), :]
        for o in range(1, owners):
            row = row + meta[o, pl.ds(code_rows + q, 1), :]
        at = lax.broadcasted_iota(jnp.int32, (owners * rows, 128), 0)
        pick = jnp.where(at == row, 1.0, 0.0).astype(BF16)
        halo = dot(every, pick).astype(BF16)
        return jnp.concatenate([features(q), halo[:, 0 : owners * slots]], axis=1)

    own_ext = extended(me)
    own_taps = dot(own_ext, hot[...]).astype(BF16)
    lane_me = pl.ds(pl.multiple_of(me * rows, rows), rows)
    pre = jnp.zeros((half, rows), F32)
    for k in range(tap_count):
        tap_k = own_taps[:, k * rows : (k + 1) * rows]
        pre = pre + dot(w_flat[k * half : (k + 1) * half, 0:full], tap_k)
        taps[k * full : (k + 1) * full, lane_me] = tap_k
    sig = jax.nn.sigmoid(pre)
    factor[...] = sig * (1.0 + pre * (1.0 - sig))

    def other_taps():
        def one(step, carry):
            q = brick(step)
            ext_q = extended(q)
            codes_q = meta[q]
            lane_q = pl.ds(pl.multiple_of(q * rows, rows), rows)
            for k in range(tap_count):
                taps[k * full : (k + 1) * full, lane_q] = dot(
                    ext_q, one_hot(codes_q, k)
                ).astype(BF16)
            return carry

        lax.fori_loop(1, owners, one, 0)

    down = pltpu.make_async_remote_copy(
        src_ref=g_out, dst_ref=g_in, send_sem=s_send, recv_sem=s_recv,
        device_id={"segment": jnp.maximum(seg - 1, 0)}, device_id_type=MESH)

    @pl.when(top)
    def _():
        up_buf[...] = cot_ref[0]

    @pl.when(jnp.logical_not(top))
    def _():
        other_taps()
        wait_slot(g_in, s_recv)
        up_buf[...] = g_in[...]

    up = up_buf[...].astype(F32)
    grad = (up * factor[...]).astype(BF16)
    gp[me] = grad
    for step in range(1, owners):
        copies.append(pltpu.make_async_remote_copy(
            src_ref=gp.at[me], dst_ref=gp.at[me],
            send_sem=p_send.at[step], recv_sem=p_recv.at[me],
            device_id={"brick": brick(step)}, device_id_type=MESH))
        copies[-1].start()

    for k in range(tap_count):
        gs[k * half : (k + 1) * half, :] = dot(
            grad, hot[:, k * rows : (k + 1) * rows], ((1,), (1,))
        ).astype(BF16)
    terms = dot(w_turn[...], gs[...])
    local, halo = terms[:, 0:rows], terms[:, rows:ext]
    fill = 128 - owners * slots
    if fill:
        halo = jnp.concatenate([halo, jnp.zeros((full, fill), F32)], axis=1)
    halo = halo.astype(BF16)
    for c in range(chans):
        halo_out[c] = halo[c * half : (c + 1) * half]
        part_out[c] = local[c * half : (c + 1) * half]
    for step in range(1, chans):
        c = lax.rem(ch + step, chans)
        copies.append(pltpu.make_async_remote_copy(
            src_ref=part_out.at[c], dst_ref=part_in.at[ch],
            send_sem=l_send.at[step], recv_sem=l_recv.at[ch],
            device_id={"chan": c}, device_id_type=MESH))
        copies[-1].start()
    for step in range(1, peers):
        _, b, c = peer(step)
        copies.append(pltpu.make_async_remote_copy(
            src_ref=halo_out.at[c], dst_ref=halo_in.at[mine],
            send_sem=h_send.at[step], recv_sem=h_recv.at[mine],
            device_id={"brick": b, "chan": c}, device_id_type=MESH))
        copies[-1].start()
    halo_in[mine] = halo_out[ch]
    half_own[...] = part_out[ch] + up

    row_iota = lax.broadcasted_iota(jnp.int32, (rows, 128), 0)

    def finish():
        place = jnp.concatenate(
            [jnp.where(own_list[q : q + 1, :] == row_iota, 1.0, 0.0).astype(BF16)
             for q in range(owners)], axis=1)
        for step in range(1, chans):
            c = lax.rem(ch + step, chans)
            wait_slot(part_in.at[c], l_recv.at[c])
        for step in range(1, peers):
            other, _, _ = peer(step)
            wait_slot(halo_in.at[other], h_recv.at[other])
        total = half_own[...]
        for step in range(1, chans):
            total = total + part_in[lax.rem(ch + step, chans)]
        came = []
        for q in range(owners):
            term = halo_in[q * chans].astype(F32)
            for c in range(1, chans):
                term = term + halo_in[q * chans + c].astype(F32)
            came.append(term.astype(BF16))
        total = total + dot(jnp.concatenate(came, axis=1), place, ((1,), (1,)))
        g_out[...] = total.astype(BF16)

        @pl.when(seg > 0)
        def _():
            down.start()

        out_ref[0, 0] = total.astype(BF16)

    @pl.when(top)
    def _():
        finish()
        other_taps()

    for step in range(1, owners):
        other = brick(step)
        wait_slot(gp.at[other], p_recv.at[other])
    every_grad = jnp.concatenate([gp[q] for q in range(owners)], axis=1)
    for k in range(tap_count):
        w_rows[pl.ds(k, half, stride=stride), 0:full] = dot(
            every_grad, taps[k * full : (k + 1) * full, :], ((1,), (1,))
        )
    for first in range(0, half, group):
        count = min(group, half - first)
        dw_ref[0, :, first * full : (first + count) * full] = jnp.concatenate(
            [w_rows[(first + j) * stride : (first + j) * stride + tap_count, 0:full]
             for j in range(count)], axis=1)

    @pl.when(jnp.logical_not(top))
    def _():
        finish()

    for copy in copies:
        copy.wait_send()

    @pl.when(seg > 0)
    def _():
        down.wait_send()


def shards(sizes, saved_inputs, cotangent, weights, neighbors, send_lists):
    owners, chans, segments, half, full, rows, slots, tap_count = sizes
    peers = owners * chans
    ext = rows + owners * slots
    stride = round_up(tap_count, 8)
    meta_rows = stride + round_up(owners, 8)
    dma = pltpu.SemaphoreType.DMA
    vmem = pl.BlockSpec(memory_space=pltpu.VMEM)
    return pl.pallas_call(
        functools.partial(body, sizes),
        out_shape=(
            jax.ShapeDtypeStruct((1, 1, half, rows), BF16),
            jax.ShapeDtypeStruct((1, tap_count, half * full), F32),
        ),
        in_specs=[vmem] * 5,
        out_specs=(vmem, vmem),
        scratch_shapes=[
            pltpu.VMEM((peers, half, rows), BF16),
            pltpu.VMEM((owners, meta_rows, 128), jnp.int32),
            pltpu.VMEM((half * stride, 128), F32),
            pltpu.VMEM((tap_count * half, 128), BF16),
            pltpu.VMEM((full, tap_count * half), BF16),
            pltpu.VMEM((ext, tap_count * rows), BF16),
            pltpu.VMEM((tap_count * full, owners * rows), BF16),
            pltpu.VMEM((half, rows), F32),
            pltpu.VMEM((half, rows), BF16),
            pltpu.VMEM((half, rows), BF16),
            pltpu.VMEM((half, rows), BF16),
            pltpu.VMEM((owners, half, rows), BF16),
            pltpu.VMEM((tap_count * half, ext), BF16),
            pltpu.VMEM((chans, half, 128), BF16),
            pltpu.VMEM((peers, half, 128), BF16),
            pltpu.VMEM((chans, half, rows), F32),
            pltpu.VMEM((chans, half, rows), F32),
            pltpu.VMEM((half, rows), F32),
            dma((peers,)), dma((peers,)), dma((owners,)), dma((owners,)),
            dma((owners,)), dma((owners,)), dma((peers,)), dma((peers,)),
            dma((chans,)), dma((chans,)), dma, dma,
        ],
        compiler_params=pltpu.CompilerParams(
            collective_id=0, has_side_effects=True, vmem_limit_bytes=48 * 1024 * 1024
        ),
    )(saved_inputs, cotangent, weights, neighbors, send_lists)


def solution(mesh):
    def call(saved_inputs, cotangent, weights, neighbors, send_lists):
        axes = mesh.shape
        half = saved_inputs.shape[2] // axes["chan"]
        owners, slots = send_lists.shape[2], send_lists.shape[3]
        rows = saved_inputs.shape[3] // (axes["groups"] * axes["brick"])
        sizes = (
            owners, axes["chan"], axes["segment"], half, saved_inputs.shape[2], rows, slots,
            weights.shape[1],
        )
        return jax.shard_map(
            functools.partial(shards, sizes),
            mesh=mesh,
            in_specs=(
                P("segment", None, "chan", ("groups", "brick")),
                P(None, "chan", ("groups", "brick")),
                P("segment", None, "chan"),
                P(None, None, ("groups", "brick")),
                P(None, ("groups", "brick"), None, None),
            ),
            out_specs=(
                P("segment", None, "chan", ("groups", "brick")),
                P(("groups", "segment"), None, "chan"),
            ),
            check_vma=False,
        )(saved_inputs, cotangent, weights, neighbors, send_lists)

    return call
```

```python
import functools
import math

import jax
import jax.numpy as jnp
from jax import lax
from jax.experimental import pallas as pl
from jax.experimental.pallas import tpu as pltpu
from jax.sharding import PartitionSpec as P

MESH = pl.DeviceIdType.MESH
F32 = jnp.float32
BF16 = jnp.bfloat16


def round_up(value, unit):
    return -(-value // unit) * unit


def dot(a, b, dims=((1,), (0,))):
    return lax.dot_general(a, b, (dims, ((), ())), preferred_element_type=F32)


def body(
    sizes,
    x_ref, cot_ref, w_ref, code_ref, list_ref,
    out_ref, dw_ref,
    packs, codes, listed, cot, w_in, w_rows, w_flat, w_turn, hot, taps, factor, up_buf, g_in, g_out,
    gp, g_rows, g_class, dw_rows, gs, pick_out, pick_in, halo_out, halo_in, part_out, part_in, half_own,
    in_sem, k_send, k_recv, x_send, x_recv, f_send, f_recv, p_send, p_recv, h_send, h_recv,
    l_send, l_recv, s_send, s_recv,
):
    owners, chans, segments, half, full, rows, slots, tap_count = sizes
    peers = owners * chans
    listed_count = owners * slots
    ext = rows + listed_count
    share = code_share(tap_count, chans)
    stride = round_up(tap_count, 8)
    me = lax.axis_index("brick")
    ch = lax.axis_index("chan")
    seg = lax.axis_index("segment")
    top = seg == segments - 1
    mine = me * chans + ch

    def peer(step):
        other = lax.rem(mine + step, peers)
        return other, other // chans, lax.rem(other, chans)

    def brick(step):
        return lax.rem(me + step, owners)

    def core(step):
        return lax.rem(ch + step, chans)

    copies = []

    def send(src, dst, out_sem, in_sem, device):
        copies.append(pltpu.make_async_remote_copy(
            src_ref=src, dst_ref=dst, send_sem=out_sem, recv_sem=in_sem,
            device_id=device, device_id_type=MESH))
        copies[-1].start()

    def arrived(dst, sem):
        pltpu.make_async_copy(dst, dst, sem).wait()

    barrier = pltpu.get_barrier_semaphore()
    for step in range(1, peers):
        _, b, c = peer(step)
        pl.semaphore_signal(barrier, 1, device_id={"brick": b, "chan": c}, device_id_type=MESH)

    @pl.when(seg > 0)
    def _():
        pl.semaphore_signal(barrier, 1, device_id={"segment": seg - 1}, device_id_type=MESH)

    @pl.when(seg < segments - 1)
    def _():
        pl.semaphore_signal(barrier, 1, device_id={"segment": seg + 1}, device_id_type=MESH)

    loads = [
        pltpu.make_async_copy(x_ref.at[0, 0], packs.at[mine, pl.ds(0, half)], in_sem.at[0]),
        pltpu.make_async_copy(code_ref, codes.at[pl.ds(0, tap_count)], in_sem.at[1]),
        pltpu.make_async_copy(w_ref.at[0], w_in, in_sem.at[2]),
        pltpu.make_async_copy(cot_ref.at[0], cot, in_sem.at[3]),
        pltpu.make_async_copy(list_ref.at[0, 0], listed, in_sem.at[4]),
    ]
    for load in loads:
        load.start()
    loads[4].wait()

    lanes = lax.broadcasted_iota(jnp.int32, (owners, 128), 1)
    receiver = lax.broadcasted_iota(jnp.int32, (owners, 128), 0)
    spread = jnp.concatenate([listed[...]] * (128 // slots), axis=1)
    flat = jnp.sum(jnp.where(lanes // slots == receiver, spread, 0), axis=0, keepdims=True)
    row_iota = lax.broadcasted_iota(jnp.int32, (rows, 128), 0)
    send_hot = jnp.where(flat == row_iota, 1.0, 0.0).astype(BF16)[:, 0:listed_count]
    list_rows = round_up(owners, 16)
    held = jnp.where(lanes // slots == me, spread, 0).astype(F32)
    if list_rows > owners:
        held = jnp.concatenate([held, jnp.zeros((list_rows - owners, 128), F32)], axis=0)

    for load in loads[0:2]:
        load.wait()
    packs[mine, half + share : half + share + list_rows, :] = held.astype(BF16)
    own_codes = jnp.concatenate(
        [codes[k] for k in range(tap_count)]
        + [jnp.zeros((chans * share - tap_count, 128), jnp.int32)], axis=0)
    part_codes = own_codes[0:share]
    for c in range(1, chans):
        part_codes = jnp.where(ch == c, own_codes[c * share : (c + 1) * share], part_codes)
    packs[mine, half : half + share, :] = part_codes.astype(F32).astype(BF16)
    picked = dot(packs[mine, 0:half, :], send_hot)
    picked = jnp.concatenate([picked, jnp.zeros((half, 128 - listed_count), F32)], axis=1) if (
        listed_count < 128) else picked
    picked = jnp.concatenate([picked, jnp.zeros((128 - half, 128), F32)], axis=0)
    picked = jnp.transpose(picked)
    for q in range(owners):
        pick_out[q] = picked[q * slots : (q + 1) * slots]

    neighbours = (
        peers - 1 + jnp.where(seg > 0, 1, 0) + jnp.where(seg < segments - 1, 1, 0)
    )
    pl.semaphore_wait(barrier, neighbours)

    for step in range(1, peers):
        _, b, c = peer(step)
        send(pick_out.at[b], pick_in.at[mine], k_send.at[step], k_recv.at[mine],
             {"brick": b, "chan": c})
    for step in range(1, chans):
        send(packs.at[mine], packs.at[mine], f_send.at[step], f_recv.at[mine],
             {"chan": core(step)})
    for step in range(1, owners):
        send(packs.at[mine], packs.at[mine], x_send.at[step], x_recv.at[me],
             {"brick": brick(step)})
    pick_in[mine] = pick_out[me]

    loads[2].wait()
    group = math.lcm(full, 128) // full
    for first in range(0, half, group):
        block = w_in[:, first * full : (first + group) * full].astype(F32)
        for j in range(group):
            at = (first + j) * stride
            w_rows[at : at + tap_count, 0:full] = block[:, j * full : (j + 1) * full]
    for k in range(tap_count):
        w_flat[k * half : (k + 1) * half, :] = (
            w_rows[pl.ds(k, half, stride=stride), :].astype(BF16)
        )
    w_turn[...] = jnp.transpose(w_flat[:, 0:full].astype(F32)).astype(BF16)

    ext_iota = lax.broadcasted_iota(jnp.int32, (ext, rows), 0)

    def one_hot(codes_of, k):
        return jnp.where(codes_of[k : k + 1, :] == ext_iota, 1.0, 0.0).astype(BF16)

    for k in range(tap_count):
        hot[:, k * rows : (k + 1) * rows] = one_hot(own_codes, k)

    def features(q):
        return jnp.concatenate([packs[q * chans + c, 0:half, :] for c in range(chans)], axis=0)

    for step in range(1, chans):
        other = me * chans + core(step)
        arrived(packs.at[other], f_recv.at[other])
    for step in range(1, peers):
        other, _, _ = peer(step)
        arrived(pick_in.at[other], k_recv.at[other])
    own_halo = jnp.concatenate(
        [jnp.transpose(jnp.concatenate(
            [pick_in[q * chans + c] for q in range(owners)], axis=0))[0:half]
         for c in range(chans)], axis=0).astype(BF16)
    own_ext = jnp.concatenate([features(me), own_halo], axis=1)
    own_taps = dot(own_ext, hot[...]).astype(BF16)
    lane_me = pl.ds(pl.multiple_of(me * rows, rows), rows)
    pre = jnp.zeros((half, rows), F32)
    for k in range(tap_count):
        tap_k = own_taps[:, k * rows : (k + 1) * rows]
        pre = pre + dot(w_flat[k * half : (k + 1) * half, 0:full], tap_k)
        taps[k * full : (k + 1) * full, lane_me] = tap_k
    sig = jax.nn.sigmoid(pre)
    factor[...] = sig * (1.0 + pre * (1.0 - sig))

    def forwards():
        return [
            pltpu.make_async_remote_copy(
                src_ref=packs.at[brick(step) * chans + ch],
                dst_ref=packs.at[brick(step) * chans + ch],
                send_sem=f_send.at[chans + (step - 1) * (chans - 1) + turn - 1],
                recv_sem=f_recv.at[brick(step) * chans + ch],
                device_id={"chan": core(turn)}, device_id_type=MESH)
            for step in range(1, owners) for turn in range(1, chans)
        ]

    def other_taps():
        passing = forwards()
        for step in range(1, owners):
            arrived(packs.at[brick(step) * chans + ch], x_recv.at[brick(step)])
            for turn in range(1, chans):
                passing[(step - 1) * (chans - 1) + turn - 1].start()
        for step in range(1, owners):
            for turn in range(1, chans):
                other = brick(step) * chans + core(turn)
                arrived(packs.at[other], f_recv.at[other])
        every = jnp.concatenate([features(o) for o in range(owners)], axis=1)
        at = lax.broadcasted_iota(jnp.int32, (owners * rows, 128), 0)
        list_at = half + share
        lists = packs[0, list_at : list_at + list_rows, :].astype(F32)
        for o in range(1, owners):
            lists = lists + packs[o * chans, list_at : list_at + list_rows, :].astype(F32)
        list_of = lax.broadcasted_iota(jnp.int32, (list_rows, 128), 0)
        owner_lane = lax.broadcasted_iota(jnp.int32, (1, 128), 1) // slots * rows

        def one(step, carry):
            q = brick(step)
            row = jnp.sum(jnp.where(list_of == q, lists, 0.0), axis=0, keepdims=True)
            row = row.astype(jnp.int32) + owner_lane
            pick = jnp.where(at == row, 1.0, 0.0).astype(BF16)
            halo = dot(every, pick).astype(BF16)
            ext_q = jnp.concatenate([features(q), halo[:, 0:listed_count]], axis=1)
            codes_q = jnp.concatenate(
                [packs[q * chans + c, half : half + share, :] for c in range(chans)], axis=0
            ).astype(F32).astype(jnp.int32)
            lane_q = pl.ds(pl.multiple_of(q * rows, rows), rows)
            for k in range(tap_count):
                taps[k * full : (k + 1) * full, lane_q] = dot(
                    ext_q, one_hot(codes_q, k)
                ).astype(BF16)
            return carry

        lax.fori_loop(1, owners, one, 0)
        for copy in passing:
            copy.wait_send()

    down = pltpu.make_async_remote_copy(
        src_ref=g_out, dst_ref=g_in, send_sem=s_send, recv_sem=s_recv,
        device_id={"segment": jnp.maximum(seg - 1, 0)}, device_id_type=MESH)

    loads[3].wait()

    @pl.when(top)
    def _():
        up_buf[...] = cot[...]

    @pl.when(jnp.logical_not(top))
    def _():
        other_taps()
        arrived(g_in, s_recv)
        up_buf[...] = g_in[...]

    up = up_buf[...].astype(F32)
    grad = (up * factor[...]).astype(BF16)
    gp[me] = grad
    for step in range(1, owners):
        send(gp.at[me], gp.at[me], p_send.at[step], p_recv.at[me], {"brick": brick(step)})

    for k in range(tap_count):
        gs[k * half : (k + 1) * half, :] = dot(
            grad, hot[:, k * rows : (k + 1) * rows], ((1,), (1,))
        ).astype(BF16)
    terms = dot(w_turn[...], gs[...])
    local, halo = terms[:, 0:rows], terms[:, rows:ext]
    if listed_count < 128:
        halo = jnp.concatenate([halo, jnp.zeros((full, 128 - listed_count), F32)], axis=1)
    halo = jnp.transpose(jnp.concatenate([halo, jnp.zeros((128 - full, 128), F32)], axis=0))
    for q in range(owners):
        halo_out[q] = halo[q * slots : (q + 1) * slots]
    for step in range(1, peers):
        _, b, c = peer(step)
        send(halo_out.at[b], halo_in.at[mine], h_send.at[step], h_recv.at[mine],
             {"brick": b, "chan": c})
    for c in range(chans):
        part_out[c] = local[c * half : (c + 1) * half]
    for step in range(1, chans):
        c = core(step)
        send(part_out.at[c], part_in.at[ch], l_send.at[step], l_recv.at[ch], {"chan": c})
    halo_in[mine] = halo_out[me]
    half_own[...] = part_out[ch] + up

    def finish():
        for step in range(1, chans):
            c = core(step)
            arrived(part_in.at[c], l_recv.at[c])
        for step in range(1, peers):
            other, _, _ = peer(step)
            arrived(halo_in.at[other], h_recv.at[other])
        total = half_own[...]
        for step in range(1, chans):
            total = total + part_in[core(step)]
        came = []
        for q in range(owners):
            term = halo_in[q * chans]
            for c in range(1, chans):
                term = term + halo_in[q * chans + c]
            came.append(term)
        came = jnp.transpose(jnp.concatenate(came, axis=0))
        own = came[0:half]
        for c in range(1, chans):
            own = jnp.where(ch == c, came[c * half : (c + 1) * half], own)
        total = total + dot(own.astype(BF16), send_hot, ((1,), (1,)))
        g_out[...] = total.astype(BF16)

        @pl.when(seg > 0)
        def _():
            down.start()

        out_ref[0, 0] = total.astype(BF16)

    @pl.when(top)
    def _():
        finish()
        other_taps()

    for step in range(1, owners):
        other = brick(step)
        arrived(gp.at[other], p_recv.at[other])
    for q in range(owners):
        for_q = gp[q].astype(F32)
        g_rows[q * half : (q + 1) * half, :] = for_q
    many = half // group
    step_rows = round_up(many, 8)
    for q in range(owners):
        for a in range(group):
            g_class[a * step_rows : a * step_rows + many, q * rows : (q + 1) * rows] = (
                g_rows[pl.ds(q * half + a, many, stride=group), :]
            )
    every_grad = g_class[...].astype(BF16)
    wide = group * full // 128
    for k in range(tap_count):
        block = dot(every_grad, taps[k * full : (k + 1) * full, :], ((1,), (1,)))
        for r in range(wide):
            pieces, at = [], r * 128
            while at < (r + 1) * 128:
                a, lane = at // full, at % full
                end = min((a + 1) * full, (r + 1) * 128)
                pieces.append(block[a * step_rows : (a + 1) * step_rows, lane : lane + end - at])
                at = end
            dw_rows[pl.ds(k * many * wide + r, many, stride=wide), :] = jnp.concatenate(
                pieces, axis=1)[0:many]
    for at in range(tap_count * many * wide // 4):
        dw_ref[at] = dw_rows[at * 4 : at * 4 + 4, :]

    @pl.when(jnp.logical_not(top))
    def _():
        finish()

    for copy in copies:
        copy.wait_send()

    @pl.when(seg > 0)
    def _():
        down.wait_send()


def code_share(tap_count, chans):
    return round_up(-(-tap_count // chans), 16)


def shards(sizes, saved_inputs, cotangent, weights, neighbors, send_lists):
    owners, chans, segments, half, full, rows, slots, tap_count = sizes
    peers = owners * chans
    ext = rows + owners * slots
    stride = round_up(tap_count, 8)
    share = code_share(tap_count, chans)
    group = math.lcm(full, 128) // full
    dma = pltpu.SemaphoreType.DMA
    vmem = pl.BlockSpec(memory_space=pltpu.VMEM)
    free = pl.BlockSpec(memory_space=pltpu.HBM)
    out, dw = pl.pallas_call(
        functools.partial(body, sizes),
        out_shape=(
            jax.ShapeDtypeStruct((1, 1, half, rows), BF16),
            jax.ShapeDtypeStruct((tap_count * half * full // 512, 4, 128), F32),
        ),
        in_specs=[free] * 5,
        out_specs=(vmem, vmem),
        scratch_shapes=[
            pltpu.VMEM((peers, half + share + round_up(owners, 16), 128), BF16),
            pltpu.VMEM((chans * share, 1, 128), jnp.int32),
            pltpu.VMEM((owners, slots), jnp.int32),
            pltpu.VMEM((half, rows), BF16),
            pltpu.VMEM((tap_count, half * full), BF16),
            pltpu.VMEM((half * stride, 128), F32),
            pltpu.VMEM((tap_count * half, 128), BF16),
            pltpu.VMEM((full, tap_count * half), BF16),
            pltpu.VMEM((ext, tap_count * rows), BF16),
            pltpu.VMEM((tap_count * full, owners * rows), BF16),
            pltpu.VMEM((half, rows), F32),
            pltpu.VMEM((half, rows), BF16),
            pltpu.VMEM((half, rows), BF16),
            pltpu.VMEM((half, rows), BF16),
            pltpu.VMEM((owners, half, rows), BF16),
            pltpu.VMEM((owners * half, rows), F32),
            pltpu.VMEM((group * round_up(half // group, 8), owners * rows), F32),
            pltpu.VMEM((tap_count * half * full // 128, 128), F32),
            pltpu.VMEM((tap_count * half, ext), BF16),
            pltpu.VMEM((owners, slots, 128), F32),
            pltpu.VMEM((peers, slots, 128), F32),
            pltpu.VMEM((owners, slots, 128), F32),
            pltpu.VMEM((peers, slots, 128), F32),
            pltpu.VMEM((chans, half, rows), F32),
            pltpu.VMEM((chans, half, rows), F32),
            pltpu.VMEM((half, rows), F32),
            dma((5,)), dma((peers,)), dma((peers,)), dma((owners,)), dma((owners,)),
            dma((chans + owners * chans,)), dma((peers,)),
            dma((owners,)), dma((owners,)), dma((peers,)), dma((peers,)),
            dma((chans,)), dma((chans,)), dma, dma,
        ],
        compiler_params=pltpu.CompilerParams(
            collective_id=0, has_side_effects=True, vmem_limit_bytes=63 * 1024 * 1024
        ),
    )(
        saved_inputs, cotangent, weights,
        jnp.transpose(neighbors, (1, 0, 2)), send_lists,
    )
    return out, dw.reshape(1, tap_count, half * full)


def solution(mesh):
    def call(saved_inputs, cotangent, weights, neighbors, send_lists):
        axes = mesh.shape
        half = saved_inputs.shape[2] // axes["chan"]
        owners, slots = send_lists.shape[2], send_lists.shape[3]
        rows = saved_inputs.shape[3] // (axes["groups"] * axes["brick"])
        sizes = (
            owners, axes["chan"], axes["segment"], half, saved_inputs.shape[2], rows, slots,
            weights.shape[1],
        )
        return jax.shard_map(
            functools.partial(shards, sizes),
            mesh=mesh,
            in_specs=(
                P("segment", None, "chan", ("groups", "brick")),
                P(None, "chan", ("groups", "brick")),
                P("segment", None, "chan"),
                P(None, None, ("groups", "brick")),
                P(None, ("groups", "brick"), None, None),
            ),
            out_specs=(
                P("segment", None, "chan", ("groups", "brick")),
                P(("groups", "segment"), None, "chan"),
            ),
            check_vma=False,
        )(saved_inputs, cotangent, weights, neighbors, send_lists)

    return call
```

```python
import functools
import math

import jax
import jax.numpy as jnp
from jax import lax
from jax.experimental import pallas as pl
from jax.experimental.pallas import tpu as pltpu
from jax.sharding import PartitionSpec as P

MESH = pl.DeviceIdType.MESH
F32 = jnp.float32
BF16 = jnp.bfloat16


def round_up(value, unit):
    return -(-value // unit) * unit


def dot(a, b, dims=((1,), (0,))):
    return lax.dot_general(a, b, (dims, ((), ())), preferred_element_type=F32)


def body(
    sizes,
    x_ref, cot_ref, w_ref, code_ref, list_ref,
    out_ref, dw_ref,
    packs, codes, listed, cot, w_in, w_rows, w_flat, w_turn, hot, taps, factor, up_buf,
    gp, g_rows, g_class, dw_rows, gs, pick_out, pick_in, halo_out, halo_in, part_out, part_in, half_own, low_halo, low_part,
    in_sem, k_send, k_recv, x_send, x_recv, f_send, f_recv, p_send, p_recv, h_send, h_recv,
    l_send, l_recv, lh_send, lh_recv, lp_send, lp_recv,
):
    owners, chans, segments, half, full, rows, slots, tap_count = sizes
    peers = owners * chans
    listed_count = owners * slots
    ext = rows + listed_count
    share = code_share(tap_count, chans)
    stride = round_up(tap_count, 8)
    me = lax.axis_index("brick")
    ch = lax.axis_index("chan")
    seg = lax.axis_index("segment")
    top = seg == segments - 1
    mine = me * chans + ch

    def peer(step):
        other = lax.rem(mine + step, peers)
        return other, other // chans, lax.rem(other, chans)

    def brick(step):
        return lax.rem(me + step, owners)

    def core(step):
        return lax.rem(ch + step, chans)

    copies = []

    def send(src, dst, out_sem, in_sem, device):
        copies.append(pltpu.make_async_remote_copy(
            src_ref=src, dst_ref=dst, send_sem=out_sem, recv_sem=in_sem,
            device_id=device, device_id_type=MESH))
        copies[-1].start()

    def arrived(dst, sem):
        pltpu.make_async_copy(dst, dst, sem).wait()

    barrier = pltpu.get_barrier_semaphore()
    for step in range(1, peers):
        _, b, c = peer(step)
        pl.semaphore_signal(barrier, 1, device_id={"brick": b, "chan": c}, device_id_type=MESH)

    @pl.when(seg < segments - 1)
    def _():
        for step in range(peers):
            _, b, c = peer(step)
            pl.semaphore_signal(
                barrier, 1, device_id={"segment": seg + 1, "brick": b, "chan": c},
                device_id_type=MESH)

    loads = [
        pltpu.make_async_copy(x_ref.at[0, 0], packs.at[mine, pl.ds(0, half)], in_sem.at[0]),
        pltpu.make_async_copy(code_ref, codes.at[pl.ds(0, tap_count)], in_sem.at[1]),
        pltpu.make_async_copy(w_ref.at[0], w_in, in_sem.at[2]),
        pltpu.make_async_copy(cot_ref.at[0], cot, in_sem.at[3]),
        pltpu.make_async_copy(list_ref.at[0, 0], listed, in_sem.at[4]),
    ]
    for load in loads:
        load.start()
    loads[4].wait()

    lanes = lax.broadcasted_iota(jnp.int32, (owners, 128), 1)
    receiver = lax.broadcasted_iota(jnp.int32, (owners, 128), 0)
    spread = jnp.concatenate([listed[...]] * (128 // slots), axis=1)
    flat = jnp.sum(jnp.where(lanes // slots == receiver, spread, 0), axis=0, keepdims=True)
    row_iota = lax.broadcasted_iota(jnp.int32, (rows, 128), 0)
    send_hot = jnp.where(flat == row_iota, 1.0, 0.0).astype(BF16)[:, 0:listed_count]
    list_rows = round_up(owners, 16)
    held = jnp.where(lanes // slots == me, spread, 0).astype(F32)
    if list_rows > owners:
        held = jnp.concatenate([held, jnp.zeros((list_rows - owners, 128), F32)], axis=0)

    for load in loads[0:2]:
        load.wait()
    packs[mine, half + share : half + share + list_rows, :] = held.astype(BF16)
    own_codes = jnp.concatenate(
        [codes[k] for k in range(tap_count)]
        + [jnp.zeros((chans * share - tap_count, 128), jnp.int32)], axis=0)
    part_codes = own_codes[0:share]
    for c in range(1, chans):
        part_codes = jnp.where(ch == c, own_codes[c * share : (c + 1) * share], part_codes)
    packs[mine, half : half + share, :] = part_codes.astype(F32).astype(BF16)
    picked = dot(packs[mine, 0:half, :], send_hot)
    picked = jnp.concatenate([picked, jnp.zeros((half, 128 - listed_count), F32)], axis=1) if (
        listed_count < 128) else picked
    picked = jnp.concatenate([picked, jnp.zeros((128 - half, 128), F32)], axis=0)
    picked = jnp.transpose(picked)
    for q in range(owners):
        pick_out[q] = picked[q * slots : (q + 1) * slots]

    neighbours = peers - 1 + jnp.where(seg > 0, peers, 0)
    pl.semaphore_wait(barrier, neighbours)

    for step in range(1, peers):
        _, b, c = peer(step)
        send(pick_out.at[b], pick_in.at[mine], k_send.at[step], k_recv.at[mine],
             {"brick": b, "chan": c})
    for step in range(1, chans):
        send(packs.at[mine], packs.at[mine], f_send.at[step], f_recv.at[mine],
             {"chan": core(step)})
    for step in range(1, owners):
        send(packs.at[mine], packs.at[mine], x_send.at[step], x_recv.at[me],
             {"brick": brick(step)})
    pick_in[mine] = pick_out[me]

    loads[2].wait()
    group = math.lcm(full, 128) // full
    for first in range(0, half, group):
        block = w_in[:, first * full : (first + group) * full].astype(F32)
        for j in range(group):
            at = (first + j) * stride
            w_rows[at : at + tap_count, 0:full] = block[:, j * full : (j + 1) * full]
    for k in range(tap_count):
        w_flat[k * half : (k + 1) * half, :] = (
            w_rows[pl.ds(k, half, stride=stride), :].astype(BF16)
        )
    w_turn[...] = jnp.transpose(w_flat[:, 0:full].astype(F32)).astype(BF16)

    ext_iota = lax.broadcasted_iota(jnp.int32, (ext, rows), 0)

    def one_hot(codes_of, k):
        return jnp.where(codes_of[k : k + 1, :] == ext_iota, 1.0, 0.0).astype(BF16)

    for k in range(tap_count):
        hot[:, k * rows : (k + 1) * rows] = one_hot(own_codes, k)

    def features(q):
        return jnp.concatenate([packs[q * chans + c, 0:half, :] for c in range(chans)], axis=0)

    for step in range(1, chans):
        other = me * chans + core(step)
        arrived(packs.at[other], f_recv.at[other])
    for step in range(1, peers):
        other, _, _ = peer(step)
        arrived(pick_in.at[other], k_recv.at[other])
    own_halo = jnp.concatenate(
        [jnp.transpose(jnp.concatenate(
            [pick_in[q * chans + c] for q in range(owners)], axis=0))[0:half]
         for c in range(chans)], axis=0).astype(BF16)
    own_ext = jnp.concatenate([features(me), own_halo], axis=1)
    own_taps = dot(own_ext, hot[...]).astype(BF16)
    lane_me = pl.ds(pl.multiple_of(me * rows, rows), rows)
    pre = jnp.zeros((half, rows), F32)
    for k in range(tap_count):
        tap_k = own_taps[:, k * rows : (k + 1) * rows]
        pre = pre + dot(w_flat[k * half : (k + 1) * half, 0:full], tap_k)
        taps[k * full : (k + 1) * full, lane_me] = tap_k
    sig = jax.nn.sigmoid(pre)
    factor[...] = sig * (1.0 + pre * (1.0 - sig))

    def forwards():
        return [
            pltpu.make_async_remote_copy(
                src_ref=packs.at[brick(step) * chans + ch],
                dst_ref=packs.at[brick(step) * chans + ch],
                send_sem=f_send.at[chans + (step - 1) * (chans - 1) + turn - 1],
                recv_sem=f_recv.at[brick(step) * chans + ch],
                device_id={"chan": core(turn)}, device_id_type=MESH)
            for step in range(1, owners) for turn in range(1, chans)
        ]

    def other_taps():
        passing = forwards()
        for step in range(1, owners):
            arrived(packs.at[brick(step) * chans + ch], x_recv.at[brick(step)])
            for turn in range(1, chans):
                passing[(step - 1) * (chans - 1) + turn - 1].start()
        for step in range(1, owners):
            for turn in range(1, chans):
                other = brick(step) * chans + core(turn)
                arrived(packs.at[other], f_recv.at[other])
        every = jnp.concatenate([features(o) for o in range(owners)], axis=1)
        at = lax.broadcasted_iota(jnp.int32, (owners * rows, 128), 0)
        list_at = half + share
        lists = packs[0, list_at : list_at + list_rows, :].astype(F32)
        for o in range(1, owners):
            lists = lists + packs[o * chans, list_at : list_at + list_rows, :].astype(F32)
        list_of = lax.broadcasted_iota(jnp.int32, (list_rows, 128), 0)
        owner_lane = lax.broadcasted_iota(jnp.int32, (1, 128), 1) // slots * rows

        def one(step, carry):
            q = brick(step)
            row = jnp.sum(jnp.where(list_of == q, lists, 0.0), axis=0, keepdims=True)
            row = row.astype(jnp.int32) + owner_lane
            pick = jnp.where(at == row, 1.0, 0.0).astype(BF16)
            halo = dot(every, pick).astype(BF16)
            ext_q = jnp.concatenate([features(q), halo[:, 0:listed_count]], axis=1)
            codes_q = jnp.concatenate(
                [packs[q * chans + c, half : half + share, :] for c in range(chans)], axis=0
            ).astype(F32).astype(jnp.int32)
            lane_q = pl.ds(pl.multiple_of(q * rows, rows), rows)
            for k in range(tap_count):
                taps[k * full : (k + 1) * full, lane_q] = dot(
                    ext_q, one_hot(codes_q, k)
                ).astype(BF16)
            return carry

        lax.fori_loop(1, owners, one, 0)
        for copy in passing:
            copy.wait_send()

    def low(src, dst, out_sem, in_sem, b, c):
        return pltpu.make_async_remote_copy(
            src_ref=src, dst_ref=dst, send_sem=out_sem, recv_sem=in_sem,
            device_id={"segment": jnp.maximum(seg - 1, 0), "brick": b, "chan": c},
            device_id_type=MESH)

    lows = []
    for step in range(peers):
        _, b, c = peer(step)
        lows.append(low(halo_out.at[b], low_halo.at[mine], lh_send.at[step], lh_recv.at[mine], b, c))
    lows.append(low(half_own, low_part.at[ch], lp_send.at[0], lp_recv.at[ch], me, ch))
    for step in range(1, chans):
        c = core(step)
        lows.append(low(part_out.at[c], low_part.at[ch], lp_send.at[step], lp_recv.at[ch], me, c))

    def placed(halos):
        came = []
        for q in range(owners):
            term = halos[q * chans]
            for c in range(1, chans):
                term = term + halos[q * chans + c]
            came.append(term)
        came = jnp.transpose(jnp.concatenate(came, axis=0))
        own = came[0:half]
        for c in range(1, chans):
            own = jnp.where(ch == c, came[c * half : (c + 1) * half], own)
        return dot(own.astype(BF16), send_hot, ((1,), (1,)))

    loads[3].wait()

    @pl.when(top)
    def _():
        up_buf[...] = cot[...]

    @pl.when(jnp.logical_not(top))
    def _():
        other_taps()
        for c in range(chans):
            arrived(low_part.at[c], lp_recv.at[c])
        for other in range(peers):
            arrived(low_halo.at[other], lh_recv.at[other])
        above = low_part[0]
        for c in range(1, chans):
            above = above + low_part[c]
        up_buf[...] = (above + placed(low_halo)).astype(BF16)

    up = up_buf[...].astype(F32)
    grad = (up * factor[...]).astype(BF16)
    gp[me] = grad
    for step in range(1, owners):
        send(gp.at[me], gp.at[me], p_send.at[step], p_recv.at[me], {"brick": brick(step)})

    for k in range(tap_count):
        gs[k * half : (k + 1) * half, :] = dot(
            grad, hot[:, k * rows : (k + 1) * rows], ((1,), (1,))
        ).astype(BF16)
    terms = dot(w_turn[...], gs[...])
    local, halo = terms[:, 0:rows], terms[:, rows:ext]
    if listed_count < 128:
        halo = jnp.concatenate([halo, jnp.zeros((full, 128 - listed_count), F32)], axis=1)
    halo = jnp.transpose(jnp.concatenate([halo, jnp.zeros((128 - full, 128), F32)], axis=0))
    for q in range(owners):
        halo_out[q] = halo[q * slots : (q + 1) * slots]
    for c in range(chans):
        part_out[c] = local[c * half : (c + 1) * half]
    half_own[...] = part_out[ch] + up

    @pl.when(seg > 0)
    def _():
        for copy in lows:
            copy.start()

    for step in range(1, peers):
        _, b, c = peer(step)
        send(halo_out.at[b], halo_in.at[mine], h_send.at[step], h_recv.at[mine],
             {"brick": b, "chan": c})
    for step in range(1, chans):
        c = core(step)
        send(part_out.at[c], part_in.at[ch], l_send.at[step], l_recv.at[ch], {"chan": c})
    halo_in[mine] = halo_out[me]

    @pl.when(top)
    def _():
        other_taps()

    for step in range(1, owners):
        other = brick(step)
        arrived(gp.at[other], p_recv.at[other])
    for q in range(owners):
        for_q = gp[q].astype(F32)
        g_rows[q * half : (q + 1) * half, :] = for_q
    many = half // group
    step_rows = round_up(many, 8)
    for q in range(owners):
        for a in range(group):
            g_class[a * step_rows : a * step_rows + many, q * rows : (q + 1) * rows] = (
                g_rows[pl.ds(q * half + a, many, stride=group), :]
            )
    every_grad = g_class[...].astype(BF16)
    wide = group * full // 128
    for k in range(tap_count):
        block = dot(every_grad, taps[k * full : (k + 1) * full, :], ((1,), (1,)))
        for r in range(wide):
            pieces, at = [], r * 128
            while at < (r + 1) * 128:
                a, lane = at // full, at % full
                end = min((a + 1) * full, (r + 1) * 128)
                pieces.append(block[a * step_rows : (a + 1) * step_rows, lane : lane + end - at])
                at = end
            dw_rows[pl.ds(k * many * wide + r, many, stride=wide), :] = jnp.concatenate(
                pieces, axis=1)[0:many]
    for at in range(tap_count * many * wide // 4):
        dw_ref[at] = dw_rows[at * 4 : at * 4 + 4, :]

    for step in range(1, chans):
        c = core(step)
        arrived(part_in.at[c], l_recv.at[c])
    for step in range(1, peers):
        other, _, _ = peer(step)
        arrived(halo_in.at[other], h_recv.at[other])
    total = half_own[...]
    for step in range(1, chans):
        total = total + part_in[core(step)]
    out_ref[0, 0] = (total + placed(halo_in)).astype(BF16)

    for copy in copies:
        copy.wait_send()

    @pl.when(seg > 0)
    def _():
        for copy in lows:
            copy.wait_send()


def code_share(tap_count, chans):
    return round_up(-(-tap_count // chans), 16)


def shards(sizes, saved_inputs, cotangent, weights, neighbors, send_lists):
    owners, chans, segments, half, full, rows, slots, tap_count = sizes
    peers = owners * chans
    ext = rows + owners * slots
    stride = round_up(tap_count, 8)
    share = code_share(tap_count, chans)
    group = math.lcm(full, 128) // full
    dma = pltpu.SemaphoreType.DMA
    vmem = pl.BlockSpec(memory_space=pltpu.VMEM)
    free = pl.BlockSpec(memory_space=pltpu.HBM)
    out, dw = pl.pallas_call(
        functools.partial(body, sizes),
        out_shape=(
            jax.ShapeDtypeStruct((1, 1, half, rows), BF16),
            jax.ShapeDtypeStruct((tap_count * half * full // 512, 4, 128), F32),
        ),
        in_specs=[free] * 5,
        out_specs=(vmem, vmem),
        scratch_shapes=[
            pltpu.VMEM((peers, half + share + round_up(owners, 16), 128), BF16),
            pltpu.VMEM((chans * share, 1, 128), jnp.int32),
            pltpu.VMEM((owners, slots), jnp.int32),
            pltpu.VMEM((half, rows), BF16),
            pltpu.VMEM((tap_count, half * full), BF16),
            pltpu.VMEM((half * stride, 128), F32),
            pltpu.VMEM((tap_count * half, 128), BF16),
            pltpu.VMEM((full, tap_count * half), BF16),
            pltpu.VMEM((ext, tap_count * rows), BF16),
            pltpu.VMEM((tap_count * full, owners * rows), BF16),
            pltpu.VMEM((half, rows), F32),
            pltpu.VMEM((half, rows), BF16),
            pltpu.VMEM((owners, half, rows), BF16),
            pltpu.VMEM((owners * half, rows), F32),
            pltpu.VMEM((group * round_up(half // group, 8), owners * rows), F32),
            pltpu.VMEM((tap_count * half * full // 128, 128), F32),
            pltpu.VMEM((tap_count * half, ext), BF16),
            pltpu.VMEM((owners, slots, 128), F32),
            pltpu.VMEM((peers, slots, 128), F32),
            pltpu.VMEM((owners, slots, 128), F32),
            pltpu.VMEM((peers, slots, 128), F32),
            pltpu.VMEM((chans, half, rows), F32),
            pltpu.VMEM((chans, half, rows), F32),
            pltpu.VMEM((half, rows), F32),
            pltpu.VMEM((peers, slots, 128), F32),
            pltpu.VMEM((chans, half, rows), F32),
            dma((5,)), dma((peers,)), dma((peers,)), dma((owners,)), dma((owners,)),
            dma((chans + owners * chans,)), dma((peers,)),
            dma((owners,)), dma((owners,)), dma((peers,)), dma((peers,)),
            dma((chans,)), dma((chans,)),
            dma((peers,)), dma((peers,)), dma((chans,)), dma((chans,)),
        ],
        compiler_params=pltpu.CompilerParams(
            collective_id=0, has_side_effects=True, vmem_limit_bytes=48 * 1024 * 1024
        ),
    )(
        *[pltpu.with_memory_space_constraint(v, pltpu.HBM) for v in (saved_inputs, cotangent, weights,
        jnp.transpose(neighbors, (1, 0, 2)), send_lists)]
    )
    return out, dw.reshape(1, tap_count, half * full)


def solution(mesh):
    def call(saved_inputs, cotangent, weights, neighbors, send_lists):
        axes = mesh.shape
        half = saved_inputs.shape[2] // axes["chan"]
        owners, slots = send_lists.shape[2], send_lists.shape[3]
        rows = saved_inputs.shape[3] // (axes["groups"] * axes["brick"])
        sizes = (
            owners, axes["chan"], axes["segment"], half, saved_inputs.shape[2], rows, slots,
            weights.shape[1],
        )
        return jax.shard_map(
            functools.partial(shards, sizes),
            mesh=mesh,
            in_specs=(
                P("segment", None, "chan", ("groups", "brick")),
                P(None, "chan", ("groups", "brick")),
                P("segment", None, "chan"),
                P(None, None, ("groups", "brick")),
                P(None, ("groups", "brick"), None, None),
            ),
            out_specs=(
                P("segment", None, "chan", ("groups", "brick")),
                P(("groups", "segment"), None, "chan"),
            ),
            check_vma=False,
        )(saved_inputs, cotangent, weights, neighbors, send_lists)

    return call
```

```python
import functools
import math

import jax
import jax.numpy as jnp
from jax import lax
from jax.experimental import pallas as pl
from jax.experimental.pallas import tpu as pltpu
from jax.sharding import PartitionSpec as P

MESH = pl.DeviceIdType.MESH
F32 = jnp.float32
BF16 = jnp.bfloat16


def round_up(value, unit):
    return -(-value // unit) * unit


def dot(a, b, dims=((1,), (0,))):
    return lax.dot_general(a, b, (dims, ((), ())), preferred_element_type=F32)


def body(
    sizes,
    x_ref, cot_ref, w_ref, code_ref, list_ref,
    out_ref, dw_ref,
    packs, codes, listed, cot, w_in, w_rows, w_flat, w_turn, hot, hot_turn, taps, factor, up_buf,
    gp, g_rows, g_class, dw_rows, gs, pick_out, pick_in, halo_out, halo_in, part_out, part_in, half_own, low_halo, low_part,
    in_sem, k_send, k_recv, x_send, x_recv, f_send, f_recv, p_send, p_recv, h_send, h_recv,
    l_send, l_recv, lh_send, lh_recv, lp_send, lp_recv,
):
    owners, chans, segments, half, full, rows, slots, tap_count = sizes
    peers = owners * chans
    listed_count = owners * slots
    ext = rows + listed_count
    share = code_share(tap_count, chans)
    stride = round_up(tap_count, 8)
    me = lax.axis_index("brick")
    ch = lax.axis_index("chan")
    seg = lax.axis_index("segment")
    top = seg == segments - 1
    mine = me * chans + ch

    def peer(step):
        other = lax.rem(mine + step, peers)
        return other, other // chans, lax.rem(other, chans)

    def brick(step):
        return lax.rem(me + step, owners)

    def core(step):
        return lax.rem(ch + step, chans)

    copies = []

    def send(src, dst, out_sem, in_sem, device):
        copies.append(pltpu.make_async_remote_copy(
            src_ref=src, dst_ref=dst, send_sem=out_sem, recv_sem=in_sem,
            device_id=device, device_id_type=MESH))
        copies[-1].start()

    def arrived(dst, sem):
        pltpu.make_async_copy(dst, dst, sem).wait()

    barrier = pltpu.get_barrier_semaphore()
    for step in range(1, peers):
        _, b, c = peer(step)
        pl.semaphore_signal(barrier, 1, device_id={"brick": b, "chan": c}, device_id_type=MESH)

    @pl.when(seg < segments - 1)
    def _():
        for step in range(peers):
            _, b, c = peer(step)
            pl.semaphore_signal(
                barrier, 1, device_id={"segment": seg + 1, "brick": b, "chan": c},
                device_id_type=MESH)

    loads = [
        pltpu.make_async_copy(x_ref.at[0, 0], packs.at[mine, pl.ds(0, half)], in_sem.at[0]),
        pltpu.make_async_copy(code_ref, codes.at[pl.ds(0, tap_count)], in_sem.at[1]),
        pltpu.make_async_copy(w_ref.at[0], w_in, in_sem.at[2]),
        pltpu.make_async_copy(cot_ref.at[0], cot, in_sem.at[3]),
        pltpu.make_async_copy(list_ref.at[0, 0], listed, in_sem.at[4]),
    ]
    for load in loads:
        load.start()
    loads[4].wait()

    lanes = lax.broadcasted_iota(jnp.int32, (owners, 128), 1)
    receiver = lax.broadcasted_iota(jnp.int32, (owners, 128), 0)
    spread = jnp.concatenate([listed[...]] * (128 // slots), axis=1)
    flat = jnp.sum(jnp.where(lanes // slots == receiver, spread, 0), axis=0, keepdims=True)
    row_iota = lax.broadcasted_iota(jnp.int32, (rows, 128), 0)
    send_hot = jnp.where(flat == row_iota, 1.0, 0.0).astype(BF16)[:, 0:listed_count]
    list_rows = round_up(owners, 16)
    held = jnp.where(lanes // slots == me, spread, 0).astype(F32)
    if list_rows > owners:
        held = jnp.concatenate([held, jnp.zeros((list_rows - owners, 128), F32)], axis=0)

    for load in loads[0:2]:
        load.wait()
    packs[mine, half + share : half + share + list_rows, :] = held.astype(BF16)
    own_codes = jnp.concatenate(
        [codes[k] for k in range(tap_count)]
        + [jnp.zeros((chans * share - tap_count, 128), jnp.int32)], axis=0)
    part_codes = own_codes[0:share]
    for c in range(1, chans):
        part_codes = jnp.where(ch == c, own_codes[c * share : (c + 1) * share], part_codes)
    packs[mine, half : half + share, :] = part_codes.astype(F32).astype(BF16)
    picked = dot(packs[mine, 0:half, :], send_hot)
    picked = jnp.concatenate([picked, jnp.zeros((half, 128 - listed_count), F32)], axis=1) if (
        listed_count < 128) else picked
    picked = jnp.concatenate([picked, jnp.zeros((128 - half, 128), F32)], axis=0)
    picked = jnp.transpose(picked)
    for q in range(owners):
        pick_out[q] = picked[q * slots : (q + 1) * slots]

    neighbours = peers - 1 + jnp.where(seg > 0, peers, 0)
    pl.semaphore_wait(barrier, neighbours)

    for step in range(1, peers):
        _, b, c = peer(step)
        send(pick_out.at[b], pick_in.at[mine], k_send.at[step], k_recv.at[mine],
             {"brick": b, "chan": c})
    for step in range(1, chans):
        send(packs.at[mine], packs.at[mine], f_send.at[step], f_recv.at[mine],
             {"chan": core(step)})
    for step in range(1, owners):
        send(packs.at[mine], packs.at[mine], x_send.at[step], x_recv.at[me],
             {"brick": brick(step)})
    pick_in[mine] = pick_out[me]

    loads[2].wait()
    group = math.lcm(full, 128) // full
    for first in range(0, half, group):
        block = w_in[:, first * full : (first + group) * full].astype(F32)
        for j in range(group):
            at = (first + j) * stride
            w_rows[at : at + tap_count, 0:full] = block[:, j * full : (j + 1) * full]
    for k in range(tap_count):
        w_flat[k * half : (k + 1) * half, :] = (
            w_rows[pl.ds(k, half, stride=stride), :].astype(BF16)
        )
    w_turn[...] = jnp.transpose(w_flat[:, 0:full].astype(F32)).astype(BF16)

    ext_iota = lax.broadcasted_iota(jnp.int32, (ext, rows), 0)

    def one_hot(codes_of, k):
        return jnp.where(codes_of[k : k + 1, :] == ext_iota, 1.0, 0.0).astype(BF16)

    for k in range(tap_count):
        hot[:, k * rows : (k + 1) * rows] = one_hot(own_codes, k)
    turned = jnp.concatenate(
        [own_codes, jnp.full((128 - chans * share, 128), -1, jnp.int32)], axis=0)
    turned = jnp.transpose(turned.astype(F32)).astype(jnp.int32)
    lane_iota = lax.broadcasted_iota(jnp.int32, (rows, ext), 1)
    for k in range(tap_count):
        hot_turn[k * rows : (k + 1) * rows, :] = jnp.where(
            turned[:, k : k + 1] == lane_iota, 1.0, 0.0).astype(BF16)

    def features(q):
        return jnp.concatenate([packs[q * chans + c, 0:half, :] for c in range(chans)], axis=0)

    for step in range(1, chans):
        other = me * chans + core(step)
        arrived(packs.at[other], f_recv.at[other])
    for step in range(1, peers):
        other, _, _ = peer(step)
        arrived(pick_in.at[other], k_recv.at[other])
    own_halo = jnp.concatenate(
        [jnp.transpose(jnp.concatenate(
            [pick_in[q * chans + c] for q in range(owners)], axis=0))[0:half]
         for c in range(chans)], axis=0).astype(BF16)
    own_ext = jnp.concatenate([features(me), own_halo], axis=1)
    own_taps = dot(own_ext, hot[...]).astype(BF16)
    lane_me = pl.ds(pl.multiple_of(me * rows, rows), rows)
    pre = jnp.zeros((half, rows), F32)
    for k in range(tap_count):
        tap_k = own_taps[:, k * rows : (k + 1) * rows]
        pre = pre + dot(w_flat[k * half : (k + 1) * half, 0:full], tap_k)
        taps[k * full : (k + 1) * full, lane_me] = tap_k
    sig = jax.nn.sigmoid(pre)
    factor[...] = sig * (1.0 + pre * (1.0 - sig))

    def forwards():
        return [
            pltpu.make_async_remote_copy(
                src_ref=packs.at[brick(step) * chans + ch],
                dst_ref=packs.at[brick(step) * chans + ch],
                send_sem=f_send.at[chans + (step - 1) * (chans - 1) + turn - 1],
                recv_sem=f_recv.at[brick(step) * chans + ch],
                device_id={"chan": core(turn)}, device_id_type=MESH)
            for step in range(1, owners) for turn in range(1, chans)
        ]

    def other_taps():
        passing = forwards()
        for step in range(1, owners):
            arrived(packs.at[brick(step) * chans + ch], x_recv.at[brick(step)])
            for turn in range(1, chans):
                passing[(step - 1) * (chans - 1) + turn - 1].start()
        for step in range(1, owners):
            for turn in range(1, chans):
                other = brick(step) * chans + core(turn)
                arrived(packs.at[other], f_recv.at[other])
        every = jnp.concatenate([features(o) for o in range(owners)], axis=1)
        at = lax.broadcasted_iota(jnp.int32, (owners * rows, 128), 0)
        list_at = half + share
        lists = packs[0, list_at : list_at + list_rows, :].astype(F32)
        for o in range(1, owners):
            lists = lists + packs[o * chans, list_at : list_at + list_rows, :].astype(F32)
        list_of = lax.broadcasted_iota(jnp.int32, (list_rows, 128), 0)
        owner_lane = lax.broadcasted_iota(jnp.int32, (1, 128), 1) // slots * rows

        def one(step, carry):
            q = brick(step)
            row = jnp.sum(jnp.where(list_of == q, lists, 0.0), axis=0, keepdims=True)
            row = row.astype(jnp.int32) + owner_lane
            pick = jnp.where(at == row, 1.0, 0.0).astype(BF16)
            halo = dot(every, pick).astype(BF16)
            ext_q = jnp.concatenate([features(q), halo[:, 0:listed_count]], axis=1)
            codes_q = jnp.concatenate(
                [packs[q * chans + c, half : half + share, :] for c in range(chans)], axis=0
            ).astype(F32).astype(jnp.int32)
            lane_q = pl.ds(pl.multiple_of(q * rows, rows), rows)
            for k in range(tap_count):
                taps[k * full : (k + 1) * full, lane_q] = dot(
                    ext_q, one_hot(codes_q, k)
                ).astype(BF16)
            return carry

        lax.fori_loop(1, owners, one, 0)
        for copy in passing:
            copy.wait_send()

    def low(src, dst, out_sem, in_sem, b, c):
        return pltpu.make_async_remote_copy(
            src_ref=src, dst_ref=dst, send_sem=out_sem, recv_sem=in_sem,
            device_id={"segment": jnp.maximum(seg - 1, 0), "brick": b, "chan": c},
            device_id_type=MESH)

    lows = []
    for step in range(peers):
        _, b, c = peer(step)
        lows.append(low(halo_out.at[b], low_halo.at[mine], lh_send.at[step], lh_recv.at[mine], b, c))
    lows.append(low(half_own, low_part.at[ch], lp_send.at[0], lp_recv.at[ch], me, ch))
    for step in range(1, chans):
        c = core(step)
        lows.append(low(part_out.at[c], low_part.at[ch], lp_send.at[step], lp_recv.at[ch], me, c))

    def placed(halos):
        came = []
        for q in range(owners):
            term = halos[q * chans]
            for c in range(1, chans):
                term = term + halos[q * chans + c]
            came.append(term)
        came = jnp.transpose(jnp.concatenate(came, axis=0))
        own = came[0:half]
        for c in range(1, chans):
            own = jnp.where(ch == c, came[c * half : (c + 1) * half], own)
        return dot(own.astype(BF16), send_hot, ((1,), (1,)))

    loads[3].wait()

    @pl.when(top)
    def _():
        up_buf[...] = cot[...]

    @pl.when(jnp.logical_not(top))
    def _():
        other_taps()
        for c in range(chans):
            arrived(low_part.at[c], lp_recv.at[c])
        for other in range(peers):
            arrived(low_halo.at[other], lh_recv.at[other])
        above = low_part[0]
        for c in range(1, chans):
            above = above + low_part[c]
        up_buf[...] = (above + placed(low_halo)).astype(BF16)

    up = up_buf[...].astype(F32)
    grad = (up * factor[...]).astype(BF16)
    gp[me] = grad
    for step in range(1, owners):
        send(gp.at[me], gp.at[me], p_send.at[step], p_recv.at[me], {"brick": brick(step)})

    for k in range(tap_count):
        gs[k * half : (k + 1) * half, :] = dot(
            grad, hot_turn[k * rows : (k + 1) * rows, :]
        ).astype(BF16)
    terms = dot(w_turn[...], gs[...])
    local, halo = terms[:, 0:rows], terms[:, rows:ext]
    if listed_count < 128:
        halo = jnp.concatenate([halo, jnp.zeros((full, 128 - listed_count), F32)], axis=1)
    halo = jnp.transpose(jnp.concatenate([halo, jnp.zeros((128 - full, 128), F32)], axis=0))
    for q in range(owners):
        halo_out[q] = halo[q * slots : (q + 1) * slots]
    for c in range(chans):
        part_out[c] = local[c * half : (c + 1) * half]
    half_own[...] = part_out[ch] + up

    @pl.when(seg > 0)
    def _():
        for copy in lows:
            copy.start()

    for step in range(1, peers):
        _, b, c = peer(step)
        send(halo_out.at[b], halo_in.at[mine], h_send.at[step], h_recv.at[mine],
             {"brick": b, "chan": c})
    for step in range(1, chans):
        c = core(step)
        send(part_out.at[c], part_in.at[ch], l_send.at[step], l_recv.at[ch], {"chan": c})
    halo_in[mine] = halo_out[me]

    @pl.when(top)
    def _():
        other_taps()

    for step in range(1, owners):
        other = brick(step)
        arrived(gp.at[other], p_recv.at[other])
    for q in range(owners):
        for_q = gp[q].astype(F32)
        g_rows[q * half : (q + 1) * half, :] = for_q
    many = half // group
    step_rows = round_up(many, 8)
    for q in range(owners):
        for a in range(group):
            g_class[a * step_rows : a * step_rows + many, q * rows : (q + 1) * rows] = (
                g_rows[pl.ds(q * half + a, many, stride=group), :]
            )
    every_grad = g_class[...].astype(BF16)
    wide = group * full // 128
    for k in range(tap_count):
        block = dot(every_grad, taps[k * full : (k + 1) * full, :], ((1,), (1,)))
        for r in range(wide):
            pieces, at = [], r * 128
            while at < (r + 1) * 128:
                a, lane = at // full, at % full
                end = min((a + 1) * full, (r + 1) * 128)
                pieces.append(block[a * step_rows : (a + 1) * step_rows, lane : lane + end - at])
                at = end
            dw_rows[pl.ds(k * many * wide + r, many, stride=wide), :] = jnp.concatenate(
                pieces, axis=1)[0:many]
    for at in range(tap_count * many * wide // 4):
        dw_ref[at] = dw_rows[at * 4 : at * 4 + 4, :]

    for step in range(1, chans):
        c = core(step)
        arrived(part_in.at[c], l_recv.at[c])
    for step in range(1, peers):
        other, _, _ = peer(step)
        arrived(halo_in.at[other], h_recv.at[other])
    total = half_own[...]
    for step in range(1, chans):
        total = total + part_in[core(step)]
    out_ref[0, 0] = (total + placed(halo_in)).astype(BF16)

    for copy in copies:
        copy.wait_send()

    @pl.when(seg > 0)
    def _():
        for copy in lows:
            copy.wait_send()


def code_share(tap_count, chans):
    return round_up(-(-tap_count // chans), 16)


def shards(sizes, saved_inputs, cotangent, weights, neighbors, send_lists):
    owners, chans, segments, half, full, rows, slots, tap_count = sizes
    peers = owners * chans
    ext = rows + owners * slots
    stride = round_up(tap_count, 8)
    share = code_share(tap_count, chans)
    group = math.lcm(full, 128) // full
    dma = pltpu.SemaphoreType.DMA
    vmem = pl.BlockSpec(memory_space=pltpu.VMEM)
    free = pl.BlockSpec(memory_space=pltpu.HBM)
    out, dw = pl.pallas_call(
        functools.partial(body, sizes),
        out_shape=(
            jax.ShapeDtypeStruct((1, 1, half, rows), BF16),
            jax.ShapeDtypeStruct((tap_count * half * full // 512, 4, 128), F32),
        ),
        in_specs=[free] * 5,
        out_specs=(vmem, vmem),
        scratch_shapes=[
            pltpu.VMEM((peers, half + share + round_up(owners, 16), 128), BF16),
            pltpu.VMEM((chans * share, 1, 128), jnp.int32),
            pltpu.VMEM((owners, slots), jnp.int32),
            pltpu.VMEM((half, rows), BF16),
            pltpu.VMEM((tap_count, half * full), BF16),
            pltpu.VMEM((half * stride, 128), F32),
            pltpu.VMEM((tap_count * half, 128), BF16),
            pltpu.VMEM((full, tap_count * half), BF16),
            pltpu.VMEM((ext, tap_count * rows), BF16),
            pltpu.VMEM((tap_count * rows, ext), BF16),
            pltpu.VMEM((tap_count * full, owners * rows), BF16),
            pltpu.VMEM((half, rows), F32),
            pltpu.VMEM((half, rows), BF16),
            pltpu.VMEM((owners, half, rows), BF16),
            pltpu.VMEM((owners * half, rows), F32),
            pltpu.VMEM((group * round_up(half // group, 8), owners * rows), F32),
            pltpu.VMEM((tap_count * half * full // 128, 128), F32),
            pltpu.VMEM((tap_count * half, ext), BF16),
            pltpu.VMEM((owners, slots, 128), F32),
            pltpu.VMEM((peers, slots, 128), F32),
            pltpu.VMEM((owners, slots, 128), F32),
            pltpu.VMEM((peers, slots, 128), F32),
            pltpu.VMEM((chans, half, rows), F32),
            pltpu.VMEM((chans, half, rows), F32),
            pltpu.VMEM((half, rows), F32),
            pltpu.VMEM((peers, slots, 128), F32),
            pltpu.VMEM((chans, half, rows), F32),
            dma((5,)), dma((peers,)), dma((peers,)), dma((owners,)), dma((owners,)),
            dma((chans + owners * chans,)), dma((peers,)),
            dma((owners,)), dma((owners,)), dma((peers,)), dma((peers,)),
            dma((chans,)), dma((chans,)),
            dma((peers,)), dma((peers,)), dma((chans,)), dma((chans,)),
        ],
        compiler_params=pltpu.CompilerParams(
            collective_id=0, has_side_effects=True, vmem_limit_bytes=48 * 1024 * 1024
        ),
    )(
        *[pltpu.with_memory_space_constraint(v, pltpu.HBM) for v in (saved_inputs, cotangent, weights,
        jnp.transpose(neighbors, (1, 0, 2)), send_lists)]
    )
    return out, dw.reshape(1, tap_count, half * full)


def solution(mesh):
    def call(saved_inputs, cotangent, weights, neighbors, send_lists):
        axes = mesh.shape
        half = saved_inputs.shape[2] // axes["chan"]
        owners, slots = send_lists.shape[2], send_lists.shape[3]
        rows = saved_inputs.shape[3] // (axes["groups"] * axes["brick"])
        sizes = (
            owners, axes["chan"], axes["segment"], half, saved_inputs.shape[2], rows, slots,
            weights.shape[1],
        )
        return jax.shard_map(
            functools.partial(shards, sizes),
            mesh=mesh,
            in_specs=(
                P("segment", None, "chan", ("groups", "brick")),
                P(None, "chan", ("groups", "brick")),
                P("segment", None, "chan"),
                P(None, None, ("groups", "brick")),
                P(None, ("groups", "brick"), None, None),
            ),
            out_specs=(
                P("segment", None, "chan", ("groups", "brick")),
                P(("groups", "segment"), None, "chan"),
            ),
            check_vma=False,
        )(saved_inputs, cotangent, weights, neighbors, send_lists)

    return call
```

```python
import functools
import math

import jax
import jax.numpy as jnp
from jax import lax
from jax.experimental import pallas as pl
from jax.experimental.pallas import tpu as pltpu
from jax.sharding import PartitionSpec as P

MESH = pl.DeviceIdType.MESH
F32 = jnp.float32
BF16 = jnp.bfloat16


def round_up(value, unit):
    return -(-value // unit) * unit


def dot(a, b, dims=((1,), (0,))):
    return lax.dot_general(a, b, (dims, ((), ())), preferred_element_type=F32)


def body(
    sizes,
    x_ref, cot_ref, w_ref, code_ref, list_ref,
    out_ref, dw_ref,
    packs, codes, listed, cot, w_in, w_rows, w_flat, w_turn, hot, hot_turn, taps, factor, up_buf,
    gp, g_rows, g_class, dw_rows, gs, pick_out, pick_in, halo_out, halo_in, part_out, part_in, half_own, low_halo, low_part,
    in_sem, k_send, k_recv, x_send, x_recv, f_send, f_recv, p_send, p_recv, h_send, h_recv,
    l_send, l_recv, lh_send, lh_recv, lp_send, lp_recv,
):
    owners, chans, segments, half, full, rows, slots, tap_count = sizes
    peers = owners * chans
    listed_count = owners * slots
    ext = rows + listed_count
    share = code_share(tap_count, chans)
    stride = round_up(tap_count, 8)
    me = lax.axis_index("brick")
    ch = lax.axis_index("chan")
    seg = lax.axis_index("segment")
    top = seg == segments - 1
    mine = me * chans + ch

    def peer(step):
        other = lax.rem(mine + step, peers)
        return other, other // chans, lax.rem(other, chans)

    def brick(step):
        return lax.rem(me + step, owners)

    def core(step):
        return lax.rem(ch + step, chans)

    copies = []

    def send(src, dst, out_sem, in_sem, device):
        copies.append(pltpu.make_async_remote_copy(
            src_ref=src, dst_ref=dst, send_sem=out_sem, recv_sem=in_sem,
            device_id=device, device_id_type=MESH))
        copies[-1].start()

    def arrived(dst, sem):
        pltpu.make_async_copy(dst, dst, sem).wait()

    barrier = pltpu.get_barrier_semaphore()
    for step in range(1, peers):
        _, b, c = peer(step)
        pl.semaphore_signal(barrier, 1, device_id={"brick": b, "chan": c}, device_id_type=MESH)

    @pl.when(seg < segments - 1)
    def _():
        for step in range(peers):
            _, b, c = peer(step)
            pl.semaphore_signal(
                barrier, 1, device_id={"segment": seg + 1, "brick": b, "chan": c},
                device_id_type=MESH)

    loads = [
        pltpu.make_async_copy(x_ref.at[0, 0], packs.at[mine, pl.ds(0, half)], in_sem.at[0]),
        pltpu.make_async_copy(code_ref, codes.at[pl.ds(0, tap_count)], in_sem.at[1]),
        pltpu.make_async_copy(w_ref.at[0], w_in, in_sem.at[2]),
        pltpu.make_async_copy(cot_ref.at[0], cot, in_sem.at[3]),
        pltpu.make_async_copy(list_ref.at[0, 0], listed, in_sem.at[4]),
    ]
    for load in loads:
        load.start()
    loads[4].wait()

    lanes = lax.broadcasted_iota(jnp.int32, (owners, 128), 1)
    receiver = lax.broadcasted_iota(jnp.int32, (owners, 128), 0)
    spread = jnp.concatenate([listed[...]] * (128 // slots), axis=1)
    flat = jnp.sum(jnp.where(lanes // slots == receiver, spread, 0), axis=0, keepdims=True)
    row_iota = lax.broadcasted_iota(jnp.int32, (rows, 128), 0)
    send_hot = jnp.where(flat == row_iota, 1.0, 0.0).astype(BF16)[:, 0:listed_count]
    list_rows = round_up(owners, 16)
    held = jnp.where(lanes // slots == me, spread, 0).astype(F32)
    if list_rows > owners:
        held = jnp.concatenate([held, jnp.zeros((list_rows - owners, 128), F32)], axis=0)

    for load in loads[0:2]:
        load.wait()
    packs[mine, half + share : half + share + list_rows, :] = held.astype(BF16)
    own_codes = jnp.concatenate(
        [codes[k] for k in range(tap_count)]
        + [jnp.zeros((chans * share - tap_count, 128), jnp.int32)], axis=0)
    part_codes = own_codes[0:share]
    for c in range(1, chans):
        part_codes = jnp.where(ch == c, own_codes[c * share : (c + 1) * share], part_codes)
    packs[mine, half : half + share, :] = part_codes.astype(F32).astype(BF16)
    picked = dot(packs[mine, 0:half, :], send_hot)
    picked = jnp.concatenate([picked, jnp.zeros((half, 128 - listed_count), F32)], axis=1) if (
        listed_count < 128) else picked
    picked = jnp.concatenate([picked, jnp.zeros((128 - half, 128), F32)], axis=0)
    picked = jnp.transpose(picked)
    for q in range(owners):
        pick_out[q] = picked[q * slots : (q + 1) * slots]

    neighbours = peers - 1 + jnp.where(seg > 0, peers, 0)
    pl.semaphore_wait(barrier, neighbours)

    for step in range(1, peers):
        _, b, c = peer(step)
        send(pick_out.at[b], pick_in.at[mine], k_send.at[step], k_recv.at[mine],
             {"brick": b, "chan": c})
    for step in range(1, chans):
        send(packs.at[mine], packs.at[mine], f_send.at[step], f_recv.at[mine],
             {"chan": core(step)})
    shared = [
        pltpu.make_async_remote_copy(
            src_ref=packs.at[mine], dst_ref=packs.at[mine],
            send_sem=x_send.at[step], recv_sem=x_recv.at[me],
            device_id={"brick": brick(step)}, device_id_type=MESH)
        for step in range(1, owners)
    ]
    copies.extend(shared)

    @pl.when(jnp.logical_not(top))
    def _():
        for copy in shared:
            copy.start()

    pick_in[mine] = pick_out[me]

    loads[2].wait()
    group = math.lcm(full, 128) // full
    for first in range(0, half, group):
        block = w_in[:, first * full : (first + group) * full].astype(F32)
        for j in range(group):
            at = (first + j) * stride
            w_rows[at : at + tap_count, 0:full] = block[:, j * full : (j + 1) * full]
    for k in range(tap_count):
        w_flat[k * half : (k + 1) * half, :] = (
            w_rows[pl.ds(k, half, stride=stride), :].astype(BF16)
        )
    w_turn[...] = jnp.transpose(w_flat[:, 0:full].astype(F32)).astype(BF16)

    ext_iota = lax.broadcasted_iota(jnp.int32, (ext, rows), 0)

    def one_hot(codes_of, k):
        return jnp.where(codes_of[k : k + 1, :] == ext_iota, 1.0, 0.0).astype(BF16)

    for k in range(tap_count):
        hot[:, k * rows : (k + 1) * rows] = one_hot(own_codes, k)
    turned = jnp.concatenate(
        [own_codes, jnp.full((128 - chans * share, 128), -1, jnp.int32)], axis=0)
    turned = jnp.transpose(turned.astype(F32)).astype(jnp.int32)
    lane_iota = lax.broadcasted_iota(jnp.int32, (rows, ext), 1)
    for k in range(tap_count):
        hot_turn[k * rows : (k + 1) * rows, :] = jnp.where(
            turned[:, k : k + 1] == lane_iota, 1.0, 0.0).astype(BF16)

    def features(q):
        return jnp.concatenate([packs[q * chans + c, 0:half, :] for c in range(chans)], axis=0)

    for step in range(1, chans):
        other = me * chans + core(step)
        arrived(packs.at[other], f_recv.at[other])
    for step in range(1, peers):
        other, _, _ = peer(step)
        arrived(pick_in.at[other], k_recv.at[other])

    @pl.when(top)
    def _():
        for copy in shared:
            copy.start()

    own_halo = jnp.concatenate(
        [jnp.transpose(jnp.concatenate(
            [pick_in[q * chans + c] for q in range(owners)], axis=0))[0:half]
         for c in range(chans)], axis=0).astype(BF16)
    own_ext = jnp.concatenate([features(me), own_halo], axis=1)
    own_taps = dot(own_ext, hot[...]).astype(BF16)
    lane_me = pl.ds(pl.multiple_of(me * rows, rows), rows)
    pre = jnp.zeros((half, rows), F32)
    for k in range(tap_count):
        tap_k = own_taps[:, k * rows : (k + 1) * rows]
        pre = pre + dot(w_flat[k * half : (k + 1) * half, 0:full], tap_k)
        taps[k * full : (k + 1) * full, lane_me] = tap_k
    sig = jax.nn.sigmoid(pre)
    factor[...] = sig * (1.0 + pre * (1.0 - sig))

    def forwards():
        return [
            pltpu.make_async_remote_copy(
                src_ref=packs.at[brick(step) * chans + ch],
                dst_ref=packs.at[brick(step) * chans + ch],
                send_sem=f_send.at[chans + (step - 1) * (chans - 1) + turn - 1],
                recv_sem=f_recv.at[brick(step) * chans + ch],
                device_id={"chan": core(turn)}, device_id_type=MESH)
            for step in range(1, owners) for turn in range(1, chans)
        ]

    def other_taps():
        passing = forwards()
        for step in range(1, owners):
            arrived(packs.at[brick(step) * chans + ch], x_recv.at[brick(step)])
            for turn in range(1, chans):
                passing[(step - 1) * (chans - 1) + turn - 1].start()
        for step in range(1, owners):
            for turn in range(1, chans):
                other = brick(step) * chans + core(turn)
                arrived(packs.at[other], f_recv.at[other])
        every = jnp.concatenate([features(o) for o in range(owners)], axis=1)
        at = lax.broadcasted_iota(jnp.int32, (owners * rows, 128), 0)
        list_at = half + share
        lists = packs[0, list_at : list_at + list_rows, :].astype(F32)
        for o in range(1, owners):
            lists = lists + packs[o * chans, list_at : list_at + list_rows, :].astype(F32)
        list_of = lax.broadcasted_iota(jnp.int32, (list_rows, 128), 0)
        owner_lane = lax.broadcasted_iota(jnp.int32, (1, 128), 1) // slots * rows

        def one(step, carry):
            q = brick(step)
            row = jnp.sum(jnp.where(list_of == q, lists, 0.0), axis=0, keepdims=True)
            row = row.astype(jnp.int32) + owner_lane
            pick = jnp.where(at == row, 1.0, 0.0).astype(BF16)
            halo = dot(every, pick).astype(BF16)
            ext_q = jnp.concatenate([features(q), halo[:, 0:listed_count]], axis=1)
            codes_q = jnp.concatenate(
                [packs[q * chans + c, half : half + share, :] for c in range(chans)], axis=0
            ).astype(F32).astype(jnp.int32)
            lane_q = pl.ds(pl.multiple_of(q * rows, rows), rows)
            for k in range(tap_count):
                taps[k * full : (k + 1) * full, lane_q] = dot(
                    ext_q, one_hot(codes_q, k)
                ).astype(BF16)
            return carry

        lax.fori_loop(1, owners, one, 0)
        for copy in passing:
            copy.wait_send()

    def low(src, dst, out_sem, in_sem, b, c):
        return pltpu.make_async_remote_copy(
            src_ref=src, dst_ref=dst, send_sem=out_sem, recv_sem=in_sem,
            device_id={"segment": jnp.maximum(seg - 1, 0), "brick": b, "chan": c},
            device_id_type=MESH)

    lows = []
    for step in range(peers):
        _, b, c = peer(step)
        lows.append(low(halo_out.at[b], low_halo.at[mine], lh_send.at[step], lh_recv.at[mine], b, c))
    lows.append(low(half_own, low_part.at[ch], lp_send.at[0], lp_recv.at[ch], me, ch))
    for step in range(1, chans):
        c = core(step)
        lows.append(low(part_out.at[c], low_part.at[ch], lp_send.at[step], lp_recv.at[ch], me, c))

    def placed(halos):
        came = []
        for q in range(owners):
            term = halos[q * chans]
            for c in range(1, chans):
                term = term + halos[q * chans + c]
            came.append(term)
        came = jnp.transpose(jnp.concatenate(came, axis=0))
        own = came[0:half]
        for c in range(1, chans):
            own = jnp.where(ch == c, came[c * half : (c + 1) * half], own)
        return dot(own.astype(BF16), send_hot, ((1,), (1,)))

    loads[3].wait()

    @pl.when(top)
    def _():
        up_buf[...] = cot[...]

    @pl.when(jnp.logical_not(top))
    def _():
        other_taps()
        for c in range(chans):
            arrived(low_part.at[c], lp_recv.at[c])
        for other in range(peers):
            arrived(low_halo.at[other], lh_recv.at[other])
        above = low_part[0]
        for c in range(1, chans):
            above = above + low_part[c]
        up_buf[...] = (above + placed(low_halo)).astype(BF16)

    up = up_buf[...].astype(F32)
    grad = (up * factor[...]).astype(BF16)
    gp[me] = grad
    for step in range(1, owners):
        send(gp.at[me], gp.at[me], p_send.at[step], p_recv.at[me], {"brick": brick(step)})

    for k in range(tap_count):
        gs[k * half : (k + 1) * half, :] = dot(
            grad, hot_turn[k * rows : (k + 1) * rows, :]
        ).astype(BF16)
    terms = dot(w_turn[...], gs[...])
    local, halo = terms[:, 0:rows], terms[:, rows:ext]
    if listed_count < 128:
        halo = jnp.concatenate([halo, jnp.zeros((full, 128 - listed_count), F32)], axis=1)
    halo = jnp.transpose(jnp.concatenate([halo, jnp.zeros((128 - full, 128), F32)], axis=0))
    for q in range(owners):
        halo_out[q] = halo[q * slots : (q + 1) * slots]
    for c in range(chans):
        part_out[c] = local[c * half : (c + 1) * half]
    half_own[...] = part_out[ch] + up

    @pl.when(seg > 0)
    def _():
        for copy in lows:
            copy.start()

    for step in range(1, peers):
        _, b, c = peer(step)
        send(halo_out.at[b], halo_in.at[mine], h_send.at[step], h_recv.at[mine],
             {"brick": b, "chan": c})
    for step in range(1, chans):
        c = core(step)
        send(part_out.at[c], part_in.at[ch], l_send.at[step], l_recv.at[ch], {"chan": c})
    halo_in[mine] = halo_out[me]

    @pl.when(top)
    def _():
        other_taps()

    for step in range(1, owners):
        other = brick(step)
        arrived(gp.at[other], p_recv.at[other])
    for q in range(owners):
        for_q = gp[q].astype(F32)
        g_rows[q * half : (q + 1) * half, :] = for_q
    many = half // group
    step_rows = round_up(many, 8)
    for q in range(owners):
        for a in range(group):
            g_class[a * step_rows : a * step_rows + many, q * rows : (q + 1) * rows] = (
                g_rows[pl.ds(q * half + a, many, stride=group), :]
            )
    every_grad = g_class[...].astype(BF16)
    wide = group * full // 128
    for k in range(tap_count):
        block = dot(every_grad, taps[k * full : (k + 1) * full, :], ((1,), (1,)))
        for r in range(wide):
            pieces, at = [], r * 128
            while at < (r + 1) * 128:
                a, lane = at // full, at % full
                end = min((a + 1) * full, (r + 1) * 128)
                pieces.append(block[a * step_rows : (a + 1) * step_rows, lane : lane + end - at])
                at = end
            dw_rows[pl.ds(k * many * wide + r, many, stride=wide), :] = jnp.concatenate(
                pieces, axis=1)[0:many]
    for at in range(tap_count * many * wide // 4):
        dw_ref[at] = dw_rows[at * 4 : at * 4 + 4, :]

    for step in range(1, chans):
        c = core(step)
        arrived(part_in.at[c], l_recv.at[c])
    for step in range(1, peers):
        other, _, _ = peer(step)
        arrived(halo_in.at[other], h_recv.at[other])
    total = half_own[...]
    for step in range(1, chans):
        total = total + part_in[core(step)]
    out_ref[0, 0] = (total + placed(halo_in)).astype(BF16)

    for copy in copies:
        copy.wait_send()

    @pl.when(seg > 0)
    def _():
        for copy in lows:
            copy.wait_send()


def code_share(tap_count, chans):
    return round_up(-(-tap_count // chans), 16)


def shards(sizes, saved_inputs, cotangent, weights, neighbors, send_lists):
    owners, chans, segments, half, full, rows, slots, tap_count = sizes
    peers = owners * chans
    ext = rows + owners * slots
    stride = round_up(tap_count, 8)
    share = code_share(tap_count, chans)
    group = math.lcm(full, 128) // full
    dma = pltpu.SemaphoreType.DMA
    vmem = pl.BlockSpec(memory_space=pltpu.VMEM)
    free = pl.BlockSpec(memory_space=pltpu.HBM)
    out, dw = pl.pallas_call(
        functools.partial(body, sizes),
        out_shape=(
            jax.ShapeDtypeStruct((1, 1, half, rows), BF16),
            jax.ShapeDtypeStruct((tap_count * half * full // 512, 4, 128), F32),
        ),
        in_specs=[free] * 5,
        out_specs=(vmem, vmem),
        scratch_shapes=[
            pltpu.VMEM((peers, half + share + round_up(owners, 16), 128), BF16),
            pltpu.VMEM((chans * share, 1, 128), jnp.int32),
            pltpu.VMEM((owners, slots), jnp.int32),
            pltpu.VMEM((half, rows), BF16),
            pltpu.VMEM((tap_count, half * full), BF16),
            pltpu.VMEM((half * stride, 128), F32),
            pltpu.VMEM((tap_count * half, 128), BF16),
            pltpu.VMEM((full, tap_count * half), BF16),
            pltpu.VMEM((ext, tap_count * rows), BF16),
            pltpu.VMEM((tap_count * rows, ext), BF16),
            pltpu.VMEM((tap_count * full, owners * rows), BF16),
            pltpu.VMEM((half, rows), F32),
            pltpu.VMEM((half, rows), BF16),
            pltpu.VMEM((owners, half, rows), BF16),
            pltpu.VMEM((owners * half, rows), F32),
            pltpu.VMEM((group * round_up(half // group, 8), owners * rows), F32),
            pltpu.VMEM((tap_count * half * full // 128, 128), F32),
            pltpu.VMEM((tap_count * half, ext), BF16),
            pltpu.VMEM((owners, slots, 128), F32),
            pltpu.VMEM((peers, slots, 128), F32),
            pltpu.VMEM((owners, slots, 128), F32),
            pltpu.VMEM((peers, slots, 128), F32),
            pltpu.VMEM((chans, half, rows), F32),
            pltpu.VMEM((chans, half, rows), F32),
            pltpu.VMEM((half, rows), F32),
            pltpu.VMEM((peers, slots, 128), F32),
            pltpu.VMEM((chans, half, rows), F32),
            dma((5,)), dma((peers,)), dma((peers,)), dma((owners,)), dma((owners,)),
            dma((chans + owners * chans,)), dma((peers,)),
            dma((owners,)), dma((owners,)), dma((peers,)), dma((peers,)),
            dma((chans,)), dma((chans,)),
            dma((peers,)), dma((peers,)), dma((chans,)), dma((chans,)),
        ],
        compiler_params=pltpu.CompilerParams(
            collective_id=0, has_side_effects=True, vmem_limit_bytes=48 * 1024 * 1024
        ),
    )(
        *[pltpu.with_memory_space_constraint(v, pltpu.HBM) for v in (saved_inputs, cotangent, weights,
        jnp.transpose(neighbors, (1, 0, 2)), send_lists)]
    )
    return out, dw.reshape(1, tap_count, half * full)


def solution(mesh):
    def call(saved_inputs, cotangent, weights, neighbors, send_lists):
        axes = mesh.shape
        half = saved_inputs.shape[2] // axes["chan"]
        owners, slots = send_lists.shape[2], send_lists.shape[3]
        rows = saved_inputs.shape[3] // (axes["groups"] * axes["brick"])
        sizes = (
            owners, axes["chan"], axes["segment"], half, saved_inputs.shape[2], rows, slots,
            weights.shape[1],
        )
        return jax.shard_map(
            functools.partial(shards, sizes),
            mesh=mesh,
            in_specs=(
                P("segment", None, "chan", ("groups", "brick")),
                P(None, "chan", ("groups", "brick")),
                P("segment", None, "chan"),
                P(None, None, ("groups", "brick")),
                P(None, ("groups", "brick"), None, None),
            ),
            out_specs=(
                P("segment", None, "chan", ("groups", "brick")),
                P(("groups", "segment"), None, "chan"),
            ),
            check_vma=False,
        )(saved_inputs, cotangent, weights, neighbors, send_lists)

    return call
```
